128 devices in a mesh: dp: 16 (over x, y), tensor: 8 (over z, core).
Axes of the slice: x: 4, y: 4, z: 4, core: 2. Of those that a mesh axis runs over, the one named last changes fastest.
Arguments:
- queries: bfloat16 [16384, 8192], P('dp', 'tensor'), may hold values from -6 to 6
- key_rows: bfloat16 [16384, 1024], P('dp', 'tensor'), may hold values from -6 to 6
- value_rows: bfloat16 [16384, 1024], P('dp', 'tensor'), may hold values from -6 to 6
- out_grad: bfloat16 [16384, 8192], P('dp', 'tensor'), may hold values from -24 to 24
- prefix: float32 [2, 64, 1024], P(None, None, 'tensor'), may hold values from -6 to 6
- lengths: int32 [32], P('dp'), may hold values from 1 to 512, as said below
- qkv_weight: bfloat16 [8192, 10240], P('dp', 'tensor'), may hold values from -0.0625 to 0.0625
Outputs:
- input_grad: bfloat16 [16384, 8192], P('dp', 'tensor')
- new_prefix: float32 [2, 64, 1024], P(None, None, 'tensor')
The draws below stay inside these ranges and needn't reach their ends.
Inputs may be any that keep to these rules, and one draw needn't show every extreme that they name: `lengths`: the longest prompt has exactly 512 live tokens.
All inputs are finite; a program needn't handle non-finite values.
Results may differ from the reference program's by a relative error of at most 0.019.
Values may be sent and summed in bfloat16 or wider, within the bound.
No kernel may reach another device: no remote copies, remote signals or barrier semaphores. Data moves between devices by JAX's collectives and lax.ppermute only.
A program may use at most 192 MiB of HBM per device.

```python
import math
import jax
import jax.numpy as jnp
from jax import lax

D = 8192
HD = 128
KVH = 8
QH = 64
PREFIX = 64
SEQ = 512
PROMPTS_DEV = 2
PROMPTS = 32
TOKENS = 16384
N_TENSOR = 8


def draw_queries(key, part):
    result = jnp.clip(jax.random.normal(jax.random.fold_in(key, 1), (TOKENS, QH * HD), jnp.float32), -6.0, 6.0)
    return result.astype(jnp.bfloat16)


def draw_prefix(key, part):
    result = jnp.clip(jax.random.normal(jax.random.fold_in(key, 3), (2, PREFIX, KVH * HD), jnp.float32), -5.0, 5.0)
    return result


def draw_lengths(key, part):
    owners = PROMPTS // PROMPTS_DEV
    spread = max(owners - 1, 1)
    device_of = jnp.arange(PROMPTS) // PROMPTS_DEV
    lowest = SEQ // 4 + SEQ * device_of // (2 * spread)
    highest = jnp.minimum(SEQ, SEQ // 3 + 2 * SEQ * device_of // (3 * spread))
    drawn = jax.random.randint(jax.random.fold_in(key, 9), (PROMPTS,), lowest, highest + 1)
    result = jnp.where(jnp.arange(PROMPTS) == PROMPTS - 1, SEQ, drawn)
    return result.astype(jnp.int32)


def level_of(key, shape, pieces, smallest, high):
    def one(axis_at, blocks):
        draws = jax.random.uniform(jax.random.fold_in(jax.random.fold_in(key, 6), axis_at), (blocks,), jnp.float32, smallest / len(pieces), high / len(pieces))
        return jnp.repeat(jnp.exp(draws), shape[axis_at] // blocks).reshape((-1,) + (1,) * (len(shape) - axis_at - 1))

    factor_of = one(*pieces[0])
    for cut in pieces[1:]:
        factor_of = factor_of * one(*cut)
    return factor_of


def gaussian(key, extent, width, bound, pieces=(), kind=jnp.bfloat16):
    entries = width * jax.random.normal(key, extent, jnp.float32)
    if pieces:
        entries = entries * level_of(key, extent, pieces, -0.22, 0.18)
    return jnp.clip(entries, -bound, bound).astype(kind)


def setup_inputs(seed: int = 0) -> dict:
    splits = jax.random.split(jax.random.key(seed), 8)
    return {
        "queries": draw_queries(jax.random.fold_in(splits[7], 71), 0),
        "key_rows": gaussian(splits[1], (TOKENS, KVH * HD), 1.0, 6.0, ((0, 16), (1, 8))),
        "value_rows": gaussian(splits[2], (TOKENS, KVH * HD), 1.0, 6.0, ((0, 16), (1, 8))),
        "out_grad": gaussian(splits[3], (TOKENS, QH * HD), 4.0, 24.0, ((0, 16), (1, 8))),
        "prefix": draw_prefix(jax.random.fold_in(splits[7], 71), 0),
        "lengths": draw_lengths(jax.random.fold_in(splits[7], 71), 0),
        "qkv_weight": gaussian(splits[6], (D, KVH * (QH // KVH + 2) * HD), D ** -0.5, 0.0625, ((0, 16), (1, 8))),
    }


rope_base = 500000.0
learning_rate = 0.1

def unrotate(gradient, positions):
    half_dim = gradient.shape[-1] // 2
    frequency = jnp.power(rope_base, -(2.0 * jnp.arange(half_dim).astype(jnp.float32)) / gradient.shape[-1])
    angles = positions.astype(jnp.float32)[:, None] * frequency[None, :]
    broadcast_shape = (gradient.shape[0],) + (1,) * (gradient.ndim - 2) + (half_dim,)
    cosine = jnp.cos(angles).reshape(broadcast_shape)
    sine_part = jnp.sin(angles).reshape(broadcast_shape)
    lower_half = gradient[..., :half_dim]
    upper_half = gradient[..., half_dim:]
    return jnp.concatenate([lower_half * cosine + upper_half * sine_part, upper_half * cosine - lower_half * sine_part], -1)

def attend_block(query_block, key_block, value_block, grad_block, prefix_keys, prefix_values):
    block_len = query_block.shape[0]
    prefix_len = prefix_keys.shape[0]
    inverse = 1.0 / math.sqrt(query_block.shape[-1])
    joined_keys = jnp.concatenate([prefix_keys, key_block], 0).astype(jnp.float32)
    joined_values = jnp.concatenate([prefix_values, value_block], 0).astype(jnp.float32)
    query_wide = query_block.astype(jnp.float32)
    grad_wide = grad_block.astype(jnp.float32)
    scores = jnp.einsum('igrd,jgd->grij', query_wide, joined_keys) * inverse
    row_index = lax.broadcasted_iota(jnp.int32, (block_len, prefix_len + block_len), 0)
    col_index = lax.broadcasted_iota(jnp.int32, (block_len, prefix_len + block_len), 1)
    visible = col_index <= row_index + prefix_len
    scores = jnp.where(visible, scores, -1e+30)
    largest = lax.optimization_barrier(jnp.max(scores, -1, keepdims=True))
    powers = jnp.exp(scores - largest)
    attn_probs = powers / lax.optimization_barrier(jnp.sum(powers, -1, keepdims=True))
    dprobs = jnp.einsum('igrd,jgd->grij', grad_wide, joined_values)
    row_term = lax.optimization_barrier(jnp.sum(attn_probs * dprobs, -1, keepdims=True))
    dscores = (attn_probs * (dprobs - row_term)).astype(jnp.bfloat16).astype(jnp.float32)
    rounded = attn_probs.astype(jnp.bfloat16).astype(jnp.float32)
    query_grad = jnp.einsum('grij,jgd->igrd', dscores, joined_keys) * inverse
    key_grad = jnp.einsum('grij,igrd->jgd', dscores, query_wide) * inverse
    value_grad = jnp.einsum('grij,igrd->jgd', rounded, grad_wide)
    return (query_grad, key_grad[prefix_len:], value_grad[prefix_len:], key_grad[:prefix_len], value_grad[:prefix_len])

def reference(queries, key_rows, value_rows, out_grad, prefix, lengths, qkv_weight):
    group_size = QH // KVH
    slot_width = KVH // N_TENSOR * (group_size + 2) * HD
    prefix_keys = prefix[0].reshape(PREFIX, KVH, HD).astype(jnp.bfloat16)
    prefix_values = prefix[1].reshape(PREFIX, KVH, HD).astype(jnp.bfloat16)
    loss_scale = jnp.float32(TOKENS) / jnp.sum(lengths).astype(jnp.float32)
    positions = jnp.arange(SEQ).astype(jnp.int32)

    def one_prompt(prefix_acc, prompt_data):
        query_part, key_part, value_part, grad_part, prompt_len = prompt_data
        live_rows = (positions < prompt_len)[:, None]
        grad_part = jnp.where(live_rows, grad_part, jnp.zeros_like(grad_part))
        query_grad, key_grad, value_grad, prefix_kgrad, prefix_vgrad = attend_block(query_part.reshape(SEQ, KVH, group_size, HD), key_part.reshape(SEQ, KVH, HD), value_part.reshape(SEQ, KVH, HD), grad_part.reshape(SEQ, KVH, group_size, HD), prefix_keys, prefix_values)
        query_grad = unrotate(query_grad, positions)
        key_grad = unrotate(key_grad, positions)
        grads = jnp.concatenate([query_grad, key_grad[:, :, None], value_grad[:, :, None]], 2)
        grads = grads.astype(jnp.bfloat16).reshape(SEQ, KVH * (group_size + 2) * HD)
        head_total = jnp.zeros((SEQ, D), jnp.float32)
        for member in range(N_TENSOR):
            partial_sum = jnp.dot(grads[:, member * slot_width:(member + 1) * slot_width], qkv_weight[:, member * slot_width:(member + 1) * slot_width].T, preferred_element_type=jnp.float32)
            partial_sum = lax.optimization_barrier(partial_sum.astype(jnp.bfloat16))
            head_total = head_total + partial_sum.astype(jnp.float32)
        grad_rows = (head_total * loss_scale).astype(jnp.bfloat16)
        prefix_acc = prefix_acc + jnp.stack([prefix_kgrad.reshape(PREFIX, KVH * HD), prefix_vgrad.reshape(PREFIX, KVH * HD)], 0)
        return (prefix_acc, grad_rows)
    prefix_grad, grad_rows = lax.scan(one_prompt, jnp.zeros((2, PREFIX, KVH * HD), jnp.float32), (queries.reshape(PROMPTS, SEQ, QH * HD), key_rows.reshape(PROMPTS, SEQ, KVH * HD), value_rows.reshape(PROMPTS, SEQ, KVH * HD), out_grad.reshape(PROMPTS, SEQ, QH * HD), lengths))
    input_grad = grad_rows.reshape(TOKENS, D)
    new_prefix = prefix - learning_rate * loss_scale * prefix_grad
    return (input_grad, new_prefix)
```

```python
import functools
import math

import jax
import jax.numpy as jnp
import numpy as np
from jax import lax
from jax.experimental import pallas as pl
from jax.experimental.pallas import tpu as pltpu
from jax.sharding import Mesh
from jax.sharding import PartitionSpec as P

learning_rate = 0.1

HD=128; GROUP=8; PREFIX=64; SEQ=512; QB=256
rope_base=500000.0

def rope_tables():
    half=HD//2
    freq=np.power(rope_base,-(2.0*np.arange(half))/HD).astype(np.float32)
    ang=(np.arange(SEQ,dtype=np.float32)[:,None]*freq[None,:]).astype(np.float64)
    cos,sin=np.cos(ang).astype(np.float32),np.sin(ang).astype(np.float32)
    wide_cos=np.concatenate([cos,cos],1)
    wide_sin=np.concatenate([sin,-sin],1)
    return cos.T.copy(),sin.T.copy(),wide_cos,wide_sin

NT=(((1,),(1,)),((),()))
NN=(((1,),(0,)),((),()))
def dot(a,b,dims): return lax.dot_general(a,b,dims,preferred_element_type=jnp.float32)

def attn_kernel(len_ref,q_ref,g_ref,k_ref,v_ref,pre_ref,cosT_ref,sinT_ref,cos_ref,sin_ref,out_ref,pg_ref,kj,vj,kT,dk_acc,dv_acc,*,prompt):
    h=pl.program_id(0)
    inverse=1.0/math.sqrt(HD)
    @pl.when(h==0)
    def _():
        kj[0:PREFIX,:]=pre_ref[0].astype(jnp.bfloat16)
        vj[0:PREFIX,:]=pre_ref[1].astype(jnp.bfloat16)
        kj[PREFIX:,:]=k_ref[...]
        vj[PREFIX:,:]=v_ref[...]
        kT[...]=jnp.transpose(kj[...].astype(jnp.float32)).astype(jnp.bfloat16)
        dk_acc[...]=jnp.zeros_like(dk_acc)
        dv_acc[...]=jnp.zeros_like(dv_acc)
    live=len_ref[prompt]
    col=pl.multiple_of(h*HD,HD)
    for b in range(SEQ//QB):
        r0=b*QB; nk=PREFIX+r0+QB
        q=q_ref[r0:r0+QB,:]
        rows=lax.broadcasted_iota(jnp.int32,(QB,HD),0)+r0
        g=jnp.where(rows<live,g_ref[r0:r0+QB,:].astype(jnp.float32),0.0).astype(jnp.bfloat16)
        s=dot(kj[0:nk,:],q,NT)
        dp=dot(vj[0:nk,:],g,NT)
        key=lax.broadcasted_iota(jnp.int32,(QB,QB),0)
        row=lax.broadcasted_iota(jnp.int32,(QB,QB),1)
        s=jnp.concatenate([s[:nk-QB],jnp.where(key<=row,s[nk-QB:],-1e30)],0)
        top=jnp.max(s,0,keepdims=True)
        e=jnp.exp((s-top)*inverse)
        p=e*(1.0/jnp.sum(e,0,keepdims=True))
        rt=jnp.sum(p*dp,0,keepdims=True)
        ds=(p*(dp-rt)).astype(jnp.bfloat16)
        pb=p.astype(jnp.bfloat16)
        dk_acc[0:nk,:]+=dot(ds,q,NN)
        dv_acc[0:nk,:]+=dot(pb,g,NN)
        dqT=dot(kT[:,0:nk],ds,NN)*inverse
        a=dqT[:HD//2]; c=dqT[HD//2:]
        co=cosT_ref[:,r0:r0+QB]; si=sinT_ref[:,r0:r0+QB]
        rot=jnp.concatenate([a*co+c*si,c*co-a*si],0)
        out_ref[r0:r0+QB,pl.ds(col,HD)]=jnp.transpose(rot).astype(jnp.bfloat16)
    @pl.when(h==GROUP-1)
    def _():
        dk=dk_acc[...]*inverse
        pg_ref[0]=dk[0:PREFIX]
        pg_ref[1]=dv_acc[0:PREFIX,:]
        d=dk[PREFIX:]
        out_ref[:,GROUP*HD:(GROUP+1)*HD]=(d*cos_ref[...]+pltpu.roll(d,HD//2,1)*sin_ref[...]).astype(jnp.bfloat16)
        out_ref[:,(GROUP+1)*HD:]=dv_acc[PREFIX:,:].astype(jnp.bfloat16)

def attention(prompt,lengths,queries,out_grad,key_rows,value_rows,prefix,tables):
    whole=lambda shape: pl.BlockSpec(shape,lambda h:(0,)*len(shape))
    return pl.pallas_call(
        functools.partial(attn_kernel,prompt=prompt),
        grid=(GROUP,),
        in_specs=[pl.BlockSpec(memory_space=pltpu.SMEM),
            pl.BlockSpec((SEQ,HD),lambda h:(prompt,h)),
            pl.BlockSpec((SEQ,HD),lambda h:(prompt,h)),
            pl.BlockSpec((SEQ,HD),lambda h:(prompt,0)),
            pl.BlockSpec((SEQ,HD),lambda h:(prompt,0)),
            whole((2,PREFIX,HD)),whole((HD//2,SEQ)),whole((HD//2,SEQ)),whole((SEQ,HD)),whole((SEQ,HD))],
        out_specs=[whole((SEQ,(GROUP+2)*HD)),whole((2,PREFIX,HD))],
        out_shape=[jax.ShapeDtypeStruct((SEQ,(GROUP+2)*HD),jnp.bfloat16),jax.ShapeDtypeStruct((2,PREFIX,HD),jnp.float32)],
        scratch_shapes=[pltpu.VMEM((PREFIX+SEQ,HD),jnp.bfloat16),pltpu.VMEM((PREFIX+SEQ,HD),jnp.bfloat16),pltpu.VMEM((HD,PREFIX+SEQ),jnp.bfloat16),
            pltpu.VMEM((PREFIX+SEQ,HD),jnp.float32),pltpu.VMEM((PREFIX+SEQ,HD),jnp.float32)],
        compiler_params=pltpu.CompilerParams(vmem_limit_bytes=40*2**20),
        cost_estimate=pl.CostEstimate(flops=5*2*8*512*576*128,bytes_accessed=4*2**20,transcendentals=8*512*576),
        name="attention_backward",
    )(lengths,queries,out_grad,key_rows,value_rows,prefix,*tables)


def multiply_kernel(place_ref, own_ref, other_ref, *refs):
    blocks, out_ref = refs[:-1], refs[-1]
    width = own_ref.shape[1]
    for at, block in enumerate(blocks):
        total = dot(own_ref[...], block[:, :width], NT) + dot(other_ref[...], block[:, width:], NT)
        out_ref[place_ref[at]] = total.astype(jnp.bfloat16)


def multiply(own, other, blocks, places):
    rows, width = own.shape
    cols = blocks[0].shape[0]
    step = min(rows, 512)
    count = len(blocks)
    return pl.pallas_call(
        multiply_kernel,
        grid=(rows // step,),
        in_specs=[
            pl.BlockSpec(memory_space=pltpu.SMEM),
            pl.BlockSpec((step, width), lambda r: (r, 0)),
            pl.BlockSpec((step, width), lambda r: (r, 0)),
        ]
        + [pl.BlockSpec((cols, 2 * width), lambda r: (0, 0))] * count,
        out_specs=pl.BlockSpec((count, step, cols), lambda r: (0, r, 0)),
        out_shape=jax.ShapeDtypeStruct((count, rows, cols), jnp.bfloat16),
        compiler_params=pltpu.CompilerParams(vmem_limit_bytes=32 * 2**20),
        cost_estimate=pl.CostEstimate(
            flops=4 * count * rows * cols * width,
            bytes_accessed=4 * rows * width + 2 * count * cols * (2 * width + rows),
            transcendentals=0,
        ),
        name="project",
    )(places, own, other, *blocks)


AXES = ("x", "y", "z", "c")


def pairs_of(move):
    def flat(x, y, z, c):
        return ((x * 4 + y) * 4 + z) * 2 + c

    found = []
    for x in range(4):
        for y in range(4):
            for z in range(4):
                for c in range(2):
                    target = move(x, y, z, c)
                    if target is not None:
                        found.append((flat(x, y, z, c), flat(*target)))
    return found


def send(array, move):
    return lax.ppermute(array, AXES, pairs_of(move))


def x_up(x, y, z, c):
    return ((x + 1) % 4, y, z, c)


def x_down(x, y, z, c):
    return ((x - 1) % 4, y, z, c)


def y_mate(x, y, z, c):
    return (x, y ^ 1, z, c)


def y_partner(x, y, z, c):
    return (x, 3 - y, z, c)


def sibling(x, y, z, c):
    return (x, y, z, 1 - c)


def home(x, y, z, c):
    half = y // 2
    return (x, 3 - y, z, c) if c == half else (x, y, z, 1 - c)


def home_rest(x, y, z, c):
    half = y // 2
    return (x, 3 - y, z, 1 - c) if c != half else None


def gather_blocks(mine):
    rows = mine.shape[0]
    from_down = send(mine, x_up)
    from_up = send(mine, x_down)
    mate = send(mine, y_mate)
    far_a = send(from_down[: rows // 2], x_up)
    far_b = send(from_up[rows // 2 :], x_down)
    far = jnp.concatenate([far_a, far_b], 0)
    mate_down = send(mate, x_up)
    mate_up = send(mate, x_down)
    mate_far = send(far, y_mate)
    return (mine, from_down, from_up, far), (mate, mate_down, mate_up, mate_far)


def body(queries, key_rows, value_rows, out_grad, prefix, lengths, qkv_weight):
    x_at, y_at, core = lax.axis_index("x"), lax.axis_index("y"), lax.axis_index("c")
    half = y_at // 2
    rows = qkv_weight.shape[0] // 2
    kept = lax.dynamic_slice_in_dim(qkv_weight, core * rows, rows, 0)
    given = lax.dynamic_slice_in_dim(qkv_weight, (1 - core) * rows, rows, 0)
    mine = jnp.concatenate([kept, send(given, sibling)], 1)
    near_blocks, mate_blocks = gather_blocks(mine)
    places = jnp.stack([x_at, (x_at + 3) % 4, (x_at + 1) % 4, (x_at + 2) % 4]).astype(jnp.int32)

    tables = tuple(jnp.asarray(t) for t in rope_tables())
    grads, prefix_terms = [], []
    for prompt in range(2):
        g, t = attention(prompt, lengths, queries, out_grad, key_rows, value_rows, prefix, tables)
        grads.append(g)
        prefix_terms.append(t)
    others = [send(g, sibling) for g in grads]
    theirs = [send(g, y_partner) for g in grads]
    their_others = [send(g, sibling) for g in theirs]

    count_row = jnp.full((8, HD), jnp.sum(lengths).astype(jnp.float32))
    terms = jnp.concatenate([(prefix_terms[0] + prefix_terms[1]).reshape(2 * PREFIX, HD), count_row], 0)
    for move in (
        lambda x, y, z, c: (x ^ 1, y, z, c),
        lambda x, y, z, c: (3 - x, y, z, c),
        lambda x, y, z, c: (x, y ^ 1, z, c),
        lambda x, y, z, c: (x, 3 - y, z, c),
    ):
        terms = terms + send(terms, move)
    loss_scale = 16384.0 / terms[2 * PREFIX, 0]
    new_prefix = prefix - learning_rate * loss_scale * terms[: 2 * PREFIX].reshape(2, PREFIX, HD)

    def reduced(own, other, blocks):
        partial = multiply(own, other, blocks, places)
        summed = lax.psum_scatter(partial, "z", scatter_dimension=0, tiled=True)[0]
        return (summed.astype(jnp.float32) * loss_scale).astype(jnp.bfloat16)

    self_own, self_other = jnp.concatenate(grads, 0), jnp.concatenate(others, 0)
    self_near = reduced(self_own, self_other, near_blocks)
    q0_near = reduced(theirs[0], their_others[0], near_blocks)
    q0_mate = reduced(theirs[0], their_others[0], mate_blocks)
    q1_near = reduced(theirs[1], their_others[1], near_blocks)
    q1_mate = reduced(theirs[1], their_others[1], mate_blocks)
    self_mate = reduced(self_own, self_other, mate_blocks)

    odd = y_at % 2 == 1

    def ordered(near, mate):
        return jnp.concatenate([jnp.where(odd, mate, near), jnp.where(odd, near, mate)], 1)

    self_part = ordered(self_near, self_mate)
    pair_part = ordered(jnp.concatenate([q0_near, q1_near], 0), jnp.concatenate([q0_mate, q1_mate], 0))
    at_home = core == half
    first = send(jnp.where(at_home, pair_part, self_part), home)
    second = send(pair_part, home_rest)
    same = jnp.where(at_home, self_part, first)
    swapped = jnp.where(at_home, first, second)
    zero, one = jnp.where(core == 0, same, swapped), jnp.where(core == 0, swapped, same)
    input_grad = jnp.stack([zero.reshape(1024, 2, 256), one.reshape(1024, 2, 256)], 2).reshape(1024, 1024)
    return (input_grad, new_prefix)


def solution(mesh):
    fine = Mesh(mesh.devices.reshape(4, 4, 4, 2), AXES)
    dp, tensor = ("x", "y"), ("z", "c")
    both = P(dp, tensor)
    return jax.shard_map(
        body,
        mesh=fine,
        in_specs=(both, both, both, both, P(None, None, tensor), P(dp), both),
        out_specs=(both, P(None, None, tensor)),
        check_vma=False,
    )
```

```python
import functools
import math

import jax
import jax.numpy as jnp
import numpy as np
from jax import lax
from jax.experimental import pallas as pl
from jax.experimental.pallas import tpu as pltpu
from jax.sharding import Mesh
from jax.sharding import PartitionSpec as P

learning_rate = 0.1

HD=128; GROUP=8; PREFIX=64; SEQ=512; QB=256
rope_base=500000.0

def rope_tables():
    half=HD//2
    freq=np.power(rope_base,-(2.0*np.arange(half))/HD).astype(np.float32)
    ang=(np.arange(SEQ,dtype=np.float32)[:,None]*freq[None,:]).astype(np.float64)
    cos,sin=np.cos(ang).astype(np.float32),np.sin(ang).astype(np.float32)
    wide_cos=np.concatenate([cos,cos],1)
    wide_sin=np.concatenate([sin,-sin],1)
    return cos.T.copy(),sin.T.copy(),wide_cos,wide_sin

NT=(((1,),(1,)),((),()))
NN=(((1,),(0,)),((),()))
def dot(a,b,dims): return lax.dot_general(a,b,dims,preferred_element_type=jnp.float32)

def attn_kernel(len_ref,q_ref,g_ref,k_ref,v_ref,pre_ref,cosT_ref,sinT_ref,cos_ref,sin_ref,out_ref,pg_ref,kj,vj,kT,dk_acc,dv_acc,*,prompt):
    h=pl.program_id(0)
    inverse=1.0/math.sqrt(HD)
    @pl.when(h==0)
    def _():
        kj[0:PREFIX,:]=pre_ref[0].astype(jnp.bfloat16)
        vj[0:PREFIX,:]=pre_ref[1].astype(jnp.bfloat16)
        kj[PREFIX:,:]=k_ref[...]
        vj[PREFIX:,:]=v_ref[...]
        kT[...]=jnp.transpose(kj[...].astype(jnp.float32)).astype(jnp.bfloat16)
        dk_acc[...]=jnp.zeros_like(dk_acc)
        dv_acc[...]=jnp.zeros_like(dv_acc)
    live=len_ref[prompt]
    col=pl.multiple_of(h*HD,HD)
    for b in range(SEQ//QB):
        r0=b*QB; nk=PREFIX+r0+QB
        q=q_ref[r0:r0+QB,:]
        rows=lax.broadcasted_iota(jnp.int32,(QB,HD),0)+r0
        g=jnp.where(rows<live,g_ref[r0:r0+QB,:].astype(jnp.float32),0.0).astype(jnp.bfloat16)
        s=dot(kj[0:nk,:],q,NT)
        dp=dot(vj[0:nk,:],g,NT)
        key=lax.broadcasted_iota(jnp.int32,(QB,QB),0)
        row=lax.broadcasted_iota(jnp.int32,(QB,QB),1)
        s=jnp.concatenate([s[:nk-QB],jnp.where(key<=row,s[nk-QB:],-1e30)],0)
        top=jnp.max(s,0,keepdims=True)
        e=jnp.exp((s-top)*inverse)
        p=e*(1.0/jnp.sum(e,0,keepdims=True))
        rt=jnp.sum(p*dp,0,keepdims=True)
        ds=(p*(dp-rt)).astype(jnp.bfloat16)
        pb=p.astype(jnp.bfloat16)
        dk_acc[0:nk,:]+=dot(ds,q,NN)
        dv_acc[0:nk,:]+=dot(pb,g,NN)
        dqT=dot(kT[:,0:nk],ds,NN)*inverse
        a=dqT[:HD//2]; c=dqT[HD//2:]
        co=cosT_ref[:,r0:r0+QB]; si=sinT_ref[:,r0:r0+QB]
        rot=jnp.concatenate([a*co+c*si,c*co-a*si],0)
        out_ref[r0:r0+QB,pl.ds(col,HD)]=jnp.transpose(rot).astype(jnp.bfloat16)
    @pl.when(h==GROUP-1)
    def _():
        dk=dk_acc[...]*inverse
        pg_ref[0]=dk[0:PREFIX]
        pg_ref[1]=dv_acc[0:PREFIX,:]
        d=dk[PREFIX:]
        out_ref[:,GROUP*HD:(GROUP+1)*HD]=(d*cos_ref[...]+pltpu.roll(d,HD//2,1)*sin_ref[...]).astype(jnp.bfloat16)
        out_ref[:,(GROUP+1)*HD:]=dv_acc[PREFIX:,:].astype(jnp.bfloat16)

def attention(prompt,lengths,queries,out_grad,key_rows,value_rows,prefix,tables):
    whole=lambda shape: pl.BlockSpec(shape,lambda h:(0,)*len(shape))
    return pl.pallas_call(
        functools.partial(attn_kernel,prompt=prompt),
        grid=(GROUP,),
        in_specs=[pl.BlockSpec(memory_space=pltpu.SMEM),
            pl.BlockSpec((SEQ,HD),lambda h:(prompt,h)),
            pl.BlockSpec((SEQ,HD),lambda h:(prompt,h)),
            pl.BlockSpec((SEQ,HD),lambda h:(prompt,0)),
            pl.BlockSpec((SEQ,HD),lambda h:(prompt,0)),
            whole((2,PREFIX,HD)),whole((HD//2,SEQ)),whole((HD//2,SEQ)),whole((SEQ,HD)),whole((SEQ,HD))],
        out_specs=[whole((SEQ,(GROUP+2)*HD)),whole((2,PREFIX,HD))],
        out_shape=[jax.ShapeDtypeStruct((SEQ,(GROUP+2)*HD),jnp.bfloat16),jax.ShapeDtypeStruct((2,PREFIX,HD),jnp.float32)],
        scratch_shapes=[pltpu.VMEM((PREFIX+SEQ,HD),jnp.bfloat16),pltpu.VMEM((PREFIX+SEQ,HD),jnp.bfloat16),pltpu.VMEM((HD,PREFIX+SEQ),jnp.bfloat16),
            pltpu.VMEM((PREFIX+SEQ,HD),jnp.float32),pltpu.VMEM((PREFIX+SEQ,HD),jnp.float32)],
        compiler_params=pltpu.CompilerParams(vmem_limit_bytes=58*2**20),
        cost_estimate=pl.CostEstimate(flops=5*2*8*512*576*128,bytes_accessed=4*2**20,transcendentals=8*512*576),
        name="attention_backward",
    )(lengths,queries,out_grad,key_rows,value_rows,prefix,*tables)

AXES = ("x", "y", "z", "c")


def pairs_of(move):
    def flat(x, y, z, c):
        return ((x * 4 + y) * 4 + z) * 2 + c

    found = []
    for x in range(4):
        for y in range(4):
            for z in range(4):
                for c in range(2):
                    target = move(x, y, z, c)
                    if target is not None:
                        found.append((flat(x, y, z, c), flat(*target)))
    return found


def send(array, move):
    return lax.ppermute(array, AXES, pairs_of(move))


def x_mate(x, y, z, c):
    return (x ^ 1, y, z, c)


def x_cross(x, y, z, c):
    return (3 - x, y, z, c)


def x_side(x, y, z, c):
    return (x ^ 1 if c == 0 else 3 - x, y, z, c)


def x_side_other(x, y, z, c):
    return (x ^ 1 if c == 1 else 3 - x, y, z, 1 - c)


def x_turn(x, y, z, c):
    return (3 - x if c == 0 else x ^ 1, y, z, c)


def y_mate(x, y, z, c):
    return (x, y ^ 1, z, c)


def y_partner(x, y, z, c):
    return (x, 3 - y, z, c)


def z_side(x, y, z, c):
    return (x, y, z ^ 1 if c == 0 else 3 - z, c)


def z_turn(x, y, z, c):
    return (x, y, 3 - z if c == 0 else z ^ 1, c)


def sibling(x, y, z, c):
    return (x, y, z, 1 - c)


def home_same(x, y, z, c):
    return (x, 3 - y, z, c) if c == y // 2 else None


def home_other(x, y, z, c):
    return (x, 3 - y, z, 1 - c) if c != y // 2 else None


def project_kernel(plan, n_arrays, *refs):
    sides, groups, outs_of = plan
    arrays, rest = refs[:n_arrays], refs[n_arrays:]
    outs, left, right, made, sems = rest[:outs_of], *rest[outs_of:]
    width = right.shape[-1]
    sem = iter(range(sems.shape[0]))

    def begin(source, target):
        copy = pltpu.make_async_copy(source, target, sems.at[next(sem)])
        copy.start()
        return copy

    side_loads = [
        [begin(arrays[at], left.at[n, :, part * width : (part + 1) * width]) for part, at in enumerate(side)]
        for n, side in enumerate(sides)
    ]
    block_loads = []
    for blocks, _ in groups:
        for pair in blocks:
            slot = len(block_loads)
            block_loads.append(
                [begin(arrays[at].at[row : row + right.shape[2]], right.at[slot, part]) for part, (at, row) in enumerate(pair)]
            )
    ready, stores, slot = set(), [], 0
    for blocks, units in groups:
        for index in range(len(blocks)):
            for copy in block_loads[slot]:
                copy.wait()
            for side, places, out, row in units:
                if side not in ready:
                    ready.add(side)
                    for copy in side_loads[side]:
                        copy.wait()
                total = dot(left[side, :, :width], right[slot, 0], NT) + dot(left[side, :, width:], right[slot, 1], NT)
                at = len(stores)
                made[at] = total.astype(jnp.bfloat16)
                place = arrays[places][index]
                stores.append(begin(made.at[at], outs[out].at[place, row : row + total.shape[0]]))
            slot += 1
    for copy in stores:
        copy.wait()


def project(groups, cols=256):
    arrays, kinds = [], []

    def slot_of(array, kind):
        for at, known in enumerate(arrays):
            if known is array:
                return at
        arrays.append(array)
        kinds.append(kind)
        return len(arrays) - 1

    sides, plan, out_rows = [], [], {}
    for blocks, units in groups:
        pairs = [tuple((slot_of(array, pl.ANY), row) for array, row in pair) for pair in blocks]
        done = []
        for (own, other), places, out, row in units:
            side = (slot_of(own, pl.ANY), slot_of(other, pl.ANY))
            if side not in sides:
                sides.append(side)
            out_rows[out] = max(out_rows.get(out, 0), row + own.shape[0])
            done.append((sides.index(side), slot_of(places, pltpu.SMEM), out, row))
        plan.append((pairs, done))
    rows, width = arrays[sides[0][0]].shape
    n_blocks = sum(len(blocks) for blocks, _ in plan)
    n_out = sum(len(blocks) * len(units) for blocks, units in plan)
    return pl.pallas_call(
        functools.partial(project_kernel, (sides, plan, len(out_rows)), len(arrays)),
        in_specs=[pl.BlockSpec(memory_space=kind) for kind in kinds],
        out_specs=[pl.BlockSpec(memory_space=pl.ANY)] * len(out_rows),
        out_shape=[jax.ShapeDtypeStruct((4, out_rows[at], cols), jnp.bfloat16) for at in sorted(out_rows)],
        scratch_shapes=[
            pltpu.VMEM((len(sides), rows, 2 * width), jnp.bfloat16),
            pltpu.VMEM((n_blocks, 2, cols, width), jnp.bfloat16),
            pltpu.VMEM((n_out, rows, cols), jnp.bfloat16),
            pltpu.SemaphoreType.DMA((2 * len(sides) + 2 * n_blocks + n_out,)),
        ],
        compiler_params=pltpu.CompilerParams(vmem_limit_bytes=58 * 2**20),
        name="project",
    )(*arrays)


def arrange_kernel(info, near, mate, near_in, mate_in, same0, same1, other0, other1, out_ref):
    at_home, near_at, own_at = info[0], info[1], info[2]
    size = near.shape[1]

    def put(value, row, base, core_at):
        col = pl.multiple_of(base * 512 + core_at * 256, 256)
        out_ref[row * size : (row + 1) * size, pl.ds(col, 256)] = value

    @pl.when(at_home == 1)
    def _():
        for row in range(2):
            put(near[row], row, near_at, own_at)
            put(mate[row], row, 1 - near_at, own_at)
            put(near_in[row], row, near_at, 1 - own_at)
            put(mate_in[row], row, 1 - near_at, 1 - own_at)

    @pl.when(at_home == 0)
    def _():
        for row, (same, other) in enumerate(((same0, other0), (same1, other1))):
            put(same[0], row, near_at, own_at)
            put(same[1], row, 1 - near_at, own_at)
            put(other[0], row, near_at, 1 - own_at)
            put(other[1], row, 1 - near_at, 1 - own_at)


def arrange(info, *parts):
    vmem = pl.BlockSpec(memory_space=pltpu.VMEM)
    return pl.pallas_call(
        arrange_kernel,
        in_specs=[pl.BlockSpec(memory_space=pltpu.SMEM)] + [vmem] * 8,
        out_specs=vmem,
        out_shape=jax.ShapeDtypeStruct((1024, 1024), jnp.bfloat16),
        compiler_params=pltpu.CompilerParams(vmem_limit_bytes=58 * 2**20),
        name="arrange",
    )(info, *parts)


def wide(array):
    return array.astype(jnp.float32)


def body(queries, key_rows, value_rows, out_grad, prefix, lengths, qkv_weight):
    gate = lax.optimization_barrier
    x_at, y_at, z_at, core = (lax.axis_index(a) for a in AXES)
    half = y_at // 2
    rows = qkv_weight.shape[0] // 2
    tables = tuple(jnp.asarray(t) for t in rope_tables())
    x_first, x_second = jnp.where(core == 0, x_at ^ 1, 3 - x_at), jnp.where(core == 0, 3 - x_at, x_at ^ 1)
    z_first, z_second = jnp.where(core == 0, z_at ^ 1, 3 - z_at), jnp.where(core == 0, 3 - z_at, z_at ^ 1)
    targets = jnp.stack([x_at, x_first, x_second, x_at ^ 2]).astype(jnp.int32)
    places = jnp.where(
        targets == z_at, 0, jnp.where(targets == z_second, 1, jnp.where(targets == z_first, 2, 3))
    ).astype(jnp.int32)

    kept = lax.dynamic_slice_in_dim(qkv_weight, core * rows, rows, 0)
    given = lax.dynamic_slice_in_dim(qkv_weight, (1 - core) * rows, rows, 0)
    kept, given, places = gate((kept, given, places))

    side_a = send(kept, x_side)
    side_b = send(given, x_side_other)
    taken = send(given, sibling)
    self0, terms0 = attention(0, lengths, queries, out_grad, key_rows, value_rows, prefix, tables)
    side_a, side_b, taken, self0, terms0, key_rows, kept = gate((side_a, side_b, taken, self0, terms0, key_rows, kept))
    mine = jnp.concatenate([kept, taken], 0)
    turned = send(jnp.concatenate([kept, taken, side_a, side_b], 0), x_turn)
    mate = send(mine, y_mate)
    pair0 = send(self0, y_partner)
    self0_other = send(self0, sibling)
    self1, terms1 = attention(1, lengths, queries, out_grad, key_rows, value_rows, prefix, tables)
    count_row = jnp.full((8, HD), jnp.sum(lengths).astype(jnp.float32))
    turned, mate, pair0, self0_other, self1, terms1, terms0, mine, self0 = gate(
        (turned, mate, pair0, self0_other, self1, terms1, terms0, mine, self0)
    )
    terms = jnp.concatenate([(terms0 + terms1).reshape(2 * PREFIX, HD), count_row], 0)
    near_blocks = [
        ((mine, 0), (mine, rows)),
        ((side_a, 0), (side_b, 0)),
        ((turned, 0), (turned, rows)),
        ((turned, 2 * rows), (turned, 3 * rows)),
    ]

    def start_unit(partial):
        return partial, send(partial[2:], z_side)

    def pass_on(held):
        partial, arrived = held
        total = (wide(partial[1]) + wide(arrived[1])).astype(jnp.bfloat16)
        return partial, arrived, send(total, z_turn)

    def finish(held):
        partial, arrived, last = held
        return ((wide(partial[0]) + wide(arrived[0]) + wide(last)) * loss_scale).astype(jnp.bfloat16)

    self1_other = send(self1, sibling)
    pair0_other = send(pair0, sibling)
    mate_side = send(mate, x_side)
    mate_turn = send(mate, x_turn)
    mate_far = send(turned[2 * rows :], y_mate)
    pair1 = send(self1, y_partner)
    both0, both1, there0 = (self0, self0_other), (self1, self1_other), (pair0, pair0_other)
    sn, p0n = project([(near_blocks, [(both0, places, 0, 0), (both1, places, 0, SEQ), (there0, places, 1, 0)])])
    mate_side, mate_turn, mate_far, pair1, there0, both0, both1, sn, p0n, mate, terms = gate(
        (mate_side, mate_turn, mate_far, pair1, there0, both0, both1, sn, p0n, mate, terms)
    )
    mate_blocks = [((array, 0), (array, rows)) for array in (mate, mate_side, mate_turn, mate_far)]
    pair1_other = send(pair1, sibling)
    sn, p0n = start_unit(sn), start_unit(p0n)
    terms = terms + send(terms, x_mate)
    p0m, sm = project([(mate_blocks, [(there0, places, 0, 0), (both0, places, 1, 0), (both1, places, 1, SEQ)])])
    pair1_other, sn, p0n, p0m, pair1, terms, sm = gate((pair1_other, sn, p0n, p0m, pair1, terms, sm))
    sn, p0n, p0m = pass_on(sn), pass_on(p0n), start_unit(p0m)
    there1 = (pair1, pair1_other)
    terms = terms + send(terms, x_cross)
    p1 = project([(near_blocks, [(there1, places, 0, 0)]), (mate_blocks, [(there1, places, 0, SEQ)])])[0]
    sn, p0n, p0m, p1, terms, sm = gate((sn, p0n, p0m, p1, terms, sm))
    p0m, p1 = pass_on(p0m), start_unit(p1)
    terms = terms + send(terms, y_mate)
    terms = terms + send(terms, y_partner)
    p0m, p1, terms, p0n, sn, sm = gate((p0m, p1, terms, p0n, sn, sm))
    loss_scale = 16384.0 / terms[2 * PREFIX, 0]
    p1, sm = pass_on(p1), start_unit(sm)
    near = finish(sn).reshape(2, SEQ, 256)
    pair0 = jnp.stack([finish(p0n), finish(p0m)])
    same0, other0 = send(pair0, home_same), send(pair0, home_other)
    near_in = send(near, sibling)
    near_in, same0, other0, p1, sm, loss_scale, near = gate((near_in, same0, other0, p1, sm, loss_scale, near))
    pair1 = finish(p1).reshape(2, SEQ, 256)
    same1, other1 = send(pair1, home_same), send(pair1, home_other)
    sm = pass_on(sm)
    mate = finish(sm).reshape(2, SEQ, 256)
    mate_in = send(mate, sibling)
    at_home = core == half
    near_at = jnp.where(at_home, y_at % 2, 1 - y_at % 2)
    info = jnp.stack([at_home.astype(jnp.int32), near_at, core]).astype(jnp.int32)
    input_grad = arrange(info, near, mate, near_in, mate_in, same0, same1, other0, other1)
    new_prefix = prefix - learning_rate * loss_scale * terms[: 2 * PREFIX].reshape(2, PREFIX, HD)
    return (input_grad, new_prefix)


def solution(mesh):
    fine = Mesh(mesh.devices.reshape(4, 4, 4, 2), AXES)
    dp, tensor = ("x", "y"), ("z", "c")
    both = P(dp, tensor)
    return jax.shard_map(
        body,
        mesh=fine,
        in_specs=(both, both, both, both, P(None, None, tensor), P(dp), both),
        out_specs=(both, P(None, None, tensor)),
        check_vma=False,
    )
```

```python
import functools
import math

import jax
import jax.numpy as jnp
import numpy as np
from jax import lax
from jax.experimental import pallas as pl
from jax.experimental.pallas import tpu as pltpu
from jax.sharding import Mesh
from jax.sharding import PartitionSpec as P

learning_rate = 0.1

HD=128; GROUP=8; PREFIX=64; SEQ=512; QB=256
rope_base=500000.0

def rope_tables():
    half=HD//2
    freq=np.power(rope_base,-(2.0*np.arange(half))/HD).astype(np.float32)
    ang=(np.arange(SEQ,dtype=np.float32)[:,None]*freq[None,:]).astype(np.float64)
    cos,sin=np.cos(ang).astype(np.float32),np.sin(ang).astype(np.float32)
    wide_cos=np.concatenate([cos,cos],1)
    wide_sin=np.concatenate([sin,-sin],1)
    return cos.T.copy(),sin.T.copy(),wide_cos,wide_sin

NT=(((1,),(1,)),((),()))
NN=(((1,),(0,)),((),()))
def dot(a,b,dims): return lax.dot_general(a,b,dims,preferred_element_type=jnp.float32)

def attn_kernel(len_ref,q_ref,g_ref,k_ref,v_ref,pre_ref,cosT_ref,sinT_ref,cos_ref,sin_ref,out_ref,pg_ref,kj,vj,kT,dk_acc,dv_acc,*,prompt):
    h=pl.program_id(0)
    inverse=1.0/math.sqrt(HD)
    @pl.when(h==0)
    def _():
        kj[0:PREFIX,:]=pre_ref[0].astype(jnp.bfloat16)
        vj[0:PREFIX,:]=pre_ref[1].astype(jnp.bfloat16)
        kj[PREFIX:,:]=k_ref[...]
        vj[PREFIX:,:]=v_ref[...]
        kT[...]=jnp.transpose(kj[...].astype(jnp.float32)).astype(jnp.bfloat16)
        dk_acc[...]=jnp.zeros_like(dk_acc)
        dv_acc[...]=jnp.zeros_like(dv_acc)
    live=len_ref[prompt]
    for b in range(SEQ//QB):
        r0=b*QB; nk=PREFIX+r0+QB
        rows=lax.broadcasted_iota(jnp.int32,(QB,HD),0)+r0
        key=lax.broadcasted_iota(jnp.int32,(QB,QB),0)
        row=lax.broadcasted_iota(jnp.int32,(QB,QB),1)
        seen=key<=row
        qs=[];gs=[];dss=[];pbs=[]
        for j in range(4):
            q=q_ref[r0:r0+QB,j*HD:(j+1)*HD]
            g=jnp.where(rows<live,g_ref[r0:r0+QB,j*HD:(j+1)*HD].astype(jnp.float32),0.0).astype(jnp.bfloat16)
            s=dot(kj[0:nk,:],q,NT)
            dp=dot(vj[0:nk,:],g,NT)
            s=jnp.concatenate([s[:nk-QB],jnp.where(seen,s[nk-QB:],-1e30)],0)
            top=jnp.max(s,0,keepdims=True)
            e=jnp.exp((s-top)*inverse)
            p=e*(1.0/jnp.sum(e,0,keepdims=True))
            rt=jnp.sum(p*dp,0,keepdims=True)
            dss.append((p*(dp-rt)).astype(jnp.bfloat16)); pbs.append(p.astype(jnp.bfloat16)); qs.append(q); gs.append(g)
        dk_acc[0:nk,:]+=dot(jnp.concatenate(dss,1),jnp.concatenate(qs,0),NN)
        dv_acc[0:nk,:]+=dot(jnp.concatenate(pbs,1),jnp.concatenate(gs,0),NN)
        for j in range(4):
            dqT=dot(kT[:,0:nk],dss[j],NN)*inverse
            a=dqT[:HD//2]; c=dqT[HD//2:]
            co=cosT_ref[:,r0:r0+QB]; si=sinT_ref[:,r0:r0+QB]
            rot=jnp.concatenate([a*co+c*si,c*co-a*si],0)
            col=pl.multiple_of((h*4+j)*HD,HD)
            out_ref[r0:r0+QB,pl.ds(col,HD)]=jnp.transpose(rot).astype(jnp.bfloat16)
    @pl.when(h==GROUP//4-1)
    def _():
        dk=dk_acc[...]*inverse
        pg_ref[0]=dk[0:PREFIX]
        pg_ref[1]=dv_acc[0:PREFIX,:]
        d=dk[PREFIX:]
        out_ref[:,GROUP*HD:(GROUP+1)*HD]=(d*cos_ref[...]+pltpu.roll(d,HD//2,1)*sin_ref[...]).astype(jnp.bfloat16)
        out_ref[:,(GROUP+1)*HD:]=dv_acc[PREFIX:,:].astype(jnp.bfloat16)

def attention(prompt,lengths,queries,out_grad,key_rows,value_rows,prefix,tables):
    whole=lambda shape: pl.BlockSpec(shape,lambda h:(0,)*len(shape))
    return pl.pallas_call(
        functools.partial(attn_kernel,prompt=prompt),
        grid=(GROUP//4,),
        in_specs=[pl.BlockSpec(memory_space=pltpu.SMEM),
            pl.BlockSpec((SEQ,4*HD),lambda h:(prompt,h)),
            pl.BlockSpec((SEQ,4*HD),lambda h:(prompt,h)),
            pl.BlockSpec((SEQ,HD),lambda h:(prompt,0)),
            pl.BlockSpec((SEQ,HD),lambda h:(prompt,0)),
            whole((2,PREFIX,HD)),whole((HD//2,SEQ)),whole((HD//2,SEQ)),whole((SEQ,HD)),whole((SEQ,HD))],
        out_specs=[whole((SEQ,(GROUP+2)*HD)),whole((2,PREFIX,HD))],
        out_shape=[jax.ShapeDtypeStruct((SEQ,(GROUP+2)*HD),jnp.bfloat16),jax.ShapeDtypeStruct((2,PREFIX,HD),jnp.float32)],
        scratch_shapes=[pltpu.VMEM((PREFIX+SEQ,HD),jnp.bfloat16),pltpu.VMEM((PREFIX+SEQ,HD),jnp.bfloat16),pltpu.VMEM((HD,PREFIX+SEQ),jnp.bfloat16),
            pltpu.VMEM((PREFIX+SEQ,HD),jnp.float32),pltpu.VMEM((PREFIX+SEQ,HD),jnp.float32)],
        compiler_params=pltpu.CompilerParams(vmem_limit_bytes=58*2**20),
        cost_estimate=pl.CostEstimate(flops=5*2*8*512*576*128,bytes_accessed=4*2**20,transcendentals=8*512*576),
        name="attention_backward",
    )(lengths,queries,out_grad,key_rows,value_rows,prefix,*tables)


AXES = ("x", "y", "z", "c")


def pairs_of(move):
    def flat(x, y, z, c):
        return ((x * 4 + y) * 4 + z) * 2 + c

    found = []
    for x in range(4):
        for y in range(4):
            for z in range(4):
                for c in range(2):
                    target = move(x, y, z, c)
                    if target is not None:
                        found.append((flat(x, y, z, c), flat(*target)))
    return found


def send(array, move):
    return lax.ppermute(array, AXES, pairs_of(move))


def x_mate(x, y, z, c):
    return (x ^ 1, y, z, c)


def x_cross(x, y, z, c):
    return (3 - x, y, z, c)


def x_side(x, y, z, c):
    return (x ^ 1 if c == 0 else 3 - x, y, z, c)


def x_side_other(x, y, z, c):
    return (x ^ 1 if c == 1 else 3 - x, y, z, 1 - c)


def x_turn(x, y, z, c):
    return (3 - x if c == 0 else x ^ 1, y, z, c)


def y_mate(x, y, z, c):
    return (x, y ^ 1, z, c)


def y_partner(x, y, z, c):
    return (x, 3 - y, z, c)


def z_side(x, y, z, c):
    return (x, y, z ^ 1 if c == 0 else 3 - z, c)


def z_turn(x, y, z, c):
    return (x, y, 3 - z if c == 0 else z ^ 1, c)


def sibling(x, y, z, c):
    return (x, y, z, 1 - c)


def home_same(x, y, z, c):
    return (x, 3 - y, z, c) if c == y // 2 else None


def home_other(x, y, z, c):
    return (x, 3 - y, z, 1 - c) if c != y // 2 else None


def project_kernel(plan, n_arrays, *refs):
    sides, groups, outs_of = plan
    arrays, rest = refs[:n_arrays], refs[n_arrays:]
    outs, left, right, made, sems = rest[: 2 * outs_of], *rest[2 * outs_of :]
    cols, width = right.shape[1], right.shape[2] // 2
    rows = left.shape[0] // len(sides)
    places = arrays[0]
    sem = iter(range(sems.shape[0]))

    def begin(source, target):
        copy = pltpu.make_async_copy(source, target, sems.at[next(sem)])
        copy.start()
        return copy

    def load_side(n):
        return [
            begin(arrays[at], left.at[n * rows : (n + 1) * rows, part * width : (part + 1) * width])
            for part, at in enumerate(sides[n])
        ]

    side_loads = load_side(0)
    blocks = [pair for group, _ in groups for pair in group]
    block_loads = [
        [
            begin(arrays[at].at[row : row + cols], right.at[slot, :, part * width : (part + 1) * width])
            for part, (at, row) in enumerate(pair)
        ]
        for slot, pair in enumerate(blocks)
    ]
    for n in range(1, len(sides)):
        side_loads += load_side(n)
    slot, done, ready, stores = 0, 0, set(), []
    for group, (first, last, cuts) in groups:
        for unit in range(first, last):
            waits = [] if unit in ready else side_loads[2 * unit : 2 * unit + 2]
            ready.add(unit)
            for index in range(len(group)):
                for copy in waits + (block_loads[slot + index] if unit == first else []):
                    copy.wait()
                waits = []
                for cut in range(0, rows, 256):
                    total = dot(left[unit * rows + cut : unit * rows + cut + 256], right[slot + index], NT)
                    made[places[index], done + cut : done + cut + 256] = total.astype(jnp.bfloat16)
            out, row = cuts[unit - first]
            for part in range(2):
                stores.append(
                    begin(made.at[2 * part : 2 * part + 2, done : done + rows], outs[2 * out + part].at[:, row : row + rows])
                )
            done += rows
        slot += len(group)
    for copy in stores:
        copy.wait()


def project(places, groups, cols=256):
    arrays, kinds = [places], [pltpu.SMEM]

    def slot_of(array):
        for at, known in enumerate(arrays):
            if known is array:
                return at
        arrays.append(array)
        kinds.append(pl.ANY)
        return len(arrays) - 1

    sides, plan, out_rows, total = [], [], {}, 0
    for blocks, lhs, cuts in groups:
        pairs = [tuple((slot_of(array), row) for array, row in pair) for pair in blocks]
        found = [(slot_of(own), slot_of(other)) for own, other in lhs]
        for side in found:
            if side not in sides:
                sides.append(side)
        for (own, _), (out, row) in zip(lhs, cuts):
            out_rows[out] = max(out_rows.get(out, 0), row + own.shape[0])
            total += own.shape[0]
        first = sides.index(found[0])
        plan.append((pairs, (first, first + len(found), cuts)))
    rows, width = arrays[sides[0][0]].shape
    n_blocks = sum(len(pairs) for pairs, _ in plan)
    hbm = pl.BlockSpec(memory_space=pl.ANY)
    out = pl.pallas_call(
        functools.partial(project_kernel, (sides, plan, len(out_rows)), len(arrays)),
        in_specs=[pl.BlockSpec(memory_space=kind) for kind in kinds],
        out_specs=[hbm] * (2 * len(out_rows)),
        out_shape=[jax.ShapeDtypeStruct((2, out_rows[at], cols), jnp.bfloat16) for at in sorted(out_rows) for _ in range(2)],
        scratch_shapes=[
            pltpu.VMEM((len(sides) * rows, 2 * width), jnp.bfloat16),
            pltpu.VMEM((n_blocks, cols, 2 * width), jnp.bfloat16),
            pltpu.VMEM((4, total, cols), jnp.bfloat16),
            pltpu.SemaphoreType.DMA((2 * len(sides) + 2 * n_blocks + 2 * (total // rows),)),
        ],
        compiler_params=pltpu.CompilerParams(vmem_limit_bytes=58 * 2**20),
        name="project",
    )(*arrays)
    return [(out[2 * at], out[2 * at + 1]) for at in range(len(out_rows))]


def arrange_kernel(info, near, mate, near_in, mate_in, same0, same1, other0, other1, out_ref):
    at_home, near_at, own_at = info[0], info[1], info[2]
    size = near.shape[1]

    def put(value, row, base, core_at):
        col = pl.multiple_of(base * 512 + core_at * 256, 256)
        out_ref[row * size : (row + 1) * size, pl.ds(col, 256)] = value

    @pl.when(at_home == 1)
    def _():
        for row in range(2):
            put(near[row], row, near_at, own_at)
            put(mate[row], row, 1 - near_at, own_at)
            put(near_in[row], row, near_at, 1 - own_at)
            put(mate_in[row], row, 1 - near_at, 1 - own_at)

    @pl.when(at_home == 0)
    def _():
        for row, (same, other) in enumerate(((same0, other0), (same1, other1))):
            put(same[0], row, near_at, own_at)
            put(same[1], row, 1 - near_at, own_at)
            put(other[0], row, near_at, 1 - own_at)
            put(other[1], row, 1 - near_at, 1 - own_at)


def arrange(info, *parts):
    vmem = pl.BlockSpec(memory_space=pltpu.VMEM)
    return pl.pallas_call(
        arrange_kernel,
        in_specs=[pl.BlockSpec(memory_space=pltpu.SMEM)] + [vmem] * 8,
        out_specs=vmem,
        out_shape=jax.ShapeDtypeStruct((1024, 1024), jnp.bfloat16),
        compiler_params=pltpu.CompilerParams(vmem_limit_bytes=58 * 2**20),
        name="arrange",
    )(info, *parts)


def wide(array):
    return array.astype(jnp.float32)


def body(queries, key_rows, value_rows, out_grad, prefix, lengths, qkv_weight):
    gate = lax.optimization_barrier
    x_at, y_at, z_at, core = (lax.axis_index(a) for a in AXES)
    half = y_at // 2
    rows = qkv_weight.shape[0] // 2
    tables = tuple(jnp.asarray(t) for t in rope_tables())
    x_first, x_second = jnp.where(core == 0, x_at ^ 1, 3 - x_at), jnp.where(core == 0, 3 - x_at, x_at ^ 1)
    z_first, z_second = jnp.where(core == 0, z_at ^ 1, 3 - z_at), jnp.where(core == 0, 3 - z_at, z_at ^ 1)
    targets = jnp.stack([x_at, x_first, x_second, x_at ^ 2]).astype(jnp.int32)
    places = jnp.where(
        targets == z_at, 0, jnp.where(targets == z_second, 1, jnp.where(targets == z_first, 2, 3))
    ).astype(jnp.int32)

    kept = lax.dynamic_slice_in_dim(qkv_weight, core * rows, rows, 0)
    given = lax.dynamic_slice_in_dim(qkv_weight, (1 - core) * rows, rows, 0)
    kept, given, places = gate((kept, given, places))

    side_a = send(kept, x_side)
    side_b = send(given, x_side_other)
    taken = send(given, sibling)
    self0, terms0 = attention(0, lengths, queries, out_grad, key_rows, value_rows, prefix, tables)
    side_a, side_b, taken, self0, terms0, key_rows, kept = gate((side_a, side_b, taken, self0, terms0, key_rows, kept))
    mine = jnp.concatenate([kept, taken], 0)
    turned = send(jnp.concatenate([kept, taken, side_a, side_b], 0), x_turn)
    mate = send(mine, y_mate)
    pair0 = send(self0, y_partner)
    self0_other = send(self0, sibling)
    self1, terms1 = attention(1, lengths, queries, out_grad, key_rows, value_rows, prefix, tables)
    count_row = jnp.full((8, HD), jnp.sum(lengths).astype(jnp.float32))
    turned, mate, pair0, self0_other, self1, terms1, terms0, mine, self0 = gate(
        (turned, mate, pair0, self0_other, self1, terms1, terms0, mine, self0)
    )
    terms = jnp.concatenate([(terms0 + terms1).reshape(2 * PREFIX, HD), count_row], 0)
    near_blocks = [
        ((mine, 0), (mine, rows)),
        ((side_a, 0), (side_b, 0)),
        ((turned, 0), (turned, rows)),
        ((turned, 2 * rows), (turned, 3 * rows)),
    ]

    def start_unit(partial):
        keep, give = partial
        return keep, send(give, z_side)

    def pass_on(held):
        partial, arrived = held
        total = (wide(partial[1]) + wide(arrived[1])).astype(jnp.bfloat16)
        return partial, arrived, send(total, z_turn)

    def finish(held):
        partial, arrived, last = held
        return ((wide(partial[0]) + wide(arrived[0]) + wide(last)) * loss_scale).astype(jnp.bfloat16)

    self1_other = send(self1, sibling)
    pair0_other = send(pair0, sibling)
    mate_side = send(mate, x_side)
    mate_turn = send(mate, x_turn)
    mate_far = send(turned[2 * rows :], y_mate)
    pair1 = send(self1, y_partner)
    both0, both1, there0 = (self0, self0_other), (self1, self1_other), (pair0, pair0_other)
    sn, p0n = project(places, [(near_blocks, [both0, both1, there0], [(0, 0), (0, SEQ), (1, 0)])])
    terms = terms + send(terms, x_mate)
    mate_side, mate_turn, mate_far, pair1, there0, both0, both1, sn, p0n, mate, terms = gate(
        (mate_side, mate_turn, mate_far, pair1, there0, both0, both1, sn, p0n, mate, terms)
    )
    mate_blocks = [((array, 0), (array, rows)) for array in (mate, mate_side, mate_turn, mate_far)]
    pair1_other = send(pair1, sibling)
    sn, p0n = start_unit(sn), start_unit(p0n)
    terms = terms + send(terms, x_cross)
    p0m, sm = project(places, [(mate_blocks, [there0, both0, both1], [(0, 0), (1, 0), (1, SEQ)])])
    pair1_other, sn, p0n, p0m, pair1, terms, sm = gate((pair1_other, sn, p0n, p0m, pair1, terms, sm))
    sn, p0n, p0m = pass_on(sn), pass_on(p0n), start_unit(p0m)
    there1 = (pair1, pair1_other)
    terms = terms + send(terms, y_mate)
    p1 = project(places, [(near_blocks, [there1], [(0, 0)]), (mate_blocks, [there1], [(0, SEQ)])])[0]
    sn, p0n, p0m, p1, terms, sm = gate((sn, p0n, p0m, p1, terms, sm))
    p0m, p1 = pass_on(p0m), start_unit(p1)
    terms = terms + send(terms, y_partner)
    p0m, p1, terms, p0n, sn, sm = gate((p0m, p1, terms, p0n, sn, sm))
    loss_scale = 16384.0 / terms[2 * PREFIX, 0]
    p1, sm = pass_on(p1), start_unit(sm)
    near = finish(sn).reshape(2, SEQ, 256)
    pair0 = jnp.stack([finish(p0n), finish(p0m)])
    same0, other0 = send(pair0, home_same), send(pair0, home_other)
    near_in = send(near, sibling)
    near_in, same0, other0, p1, sm, loss_scale, near = gate((near_in, same0, other0, p1, sm, loss_scale, near))
    pair1 = finish(p1).reshape(2, SEQ, 256)
    same1, other1 = send(pair1, home_same), send(pair1, home_other)
    sm = pass_on(sm)
    mate = finish(sm).reshape(2, SEQ, 256)
    mate_in = send(mate, sibling)
    at_home = core == half
    near_at = jnp.where(at_home, y_at % 2, 1 - y_at % 2)
    info = jnp.stack([at_home.astype(jnp.int32), near_at, core]).astype(jnp.int32)
    input_grad = arrange(info, near, mate, near_in, mate_in, same0, same1, other0, other1)
    new_prefix = prefix - learning_rate * loss_scale * terms[: 2 * PREFIX].reshape(2, PREFIX, HD)
    return (input_grad, new_prefix)


def solution(mesh):
    fine = Mesh(mesh.devices.reshape(4, 4, 4, 2), AXES)
    dp, tensor = ("x", "y"), ("z", "c")
    both = P(dp, tensor)
    return jax.shard_map(
        body,
        mesh=fine,
        in_specs=(both, both, both, both, P(None, None, tensor), P(dp), both),
        out_specs=(both, P(None, None, tensor)),
        check_vma=False,
    )
```

```python
import functools
import math

import jax
import jax.numpy as jnp
import numpy as np
from jax import lax
from jax.experimental import pallas as pl
from jax.experimental.pallas import tpu as pltpu
from jax.sharding import Mesh
from jax.sharding import PartitionSpec as P

learning_rate = 0.1

HD=128; GROUP=8; PREFIX=64; SEQ=512; QB=256
rope_base=500000.0

def rope_tables():
    half=HD//2
    freq=np.power(rope_base,-(2.0*np.arange(half))/HD).astype(np.float32)
    ang=(np.arange(SEQ,dtype=np.float32)[:,None]*freq[None,:]).astype(np.float64)
    cos,sin=np.cos(ang).astype(np.float32),np.sin(ang).astype(np.float32)
    wide_cos=np.concatenate([cos,cos],1)
    wide_sin=np.concatenate([sin,-sin],1)
    return cos.T.copy(),sin.T.copy(),wide_cos,wide_sin

NT=(((1,),(1,)),((),()))
NN=(((1,),(0,)),((),()))
def dot(a,b,dims): return lax.dot_general(a,b,dims,preferred_element_type=jnp.float32)

def attn_kernel(len_ref,q_ref,g_ref,k_ref,v_ref,pre_ref,cosT_ref,sinT_ref,cos_ref,sin_ref,out_ref,pg_ref,kj,vj,kT,dk_acc,dv_acc,*,prompt):
    h=pl.program_id(0)
    inverse=1.0/math.sqrt(HD)
    @pl.when(h==0)
    def _():
        kj[0:PREFIX,:]=pre_ref[0].astype(jnp.bfloat16)
        vj[0:PREFIX,:]=pre_ref[1].astype(jnp.bfloat16)
        kj[PREFIX:,:]=k_ref[...]
        vj[PREFIX:,:]=v_ref[...]
        kT[...]=jnp.transpose(kj[...].astype(jnp.float32)).astype(jnp.bfloat16)
        dk_acc[...]=jnp.zeros_like(dk_acc)
        dv_acc[...]=jnp.zeros_like(dv_acc)
    live=len_ref[prompt]
    for b in range(SEQ//QB):
        r0=b*QB; nk=PREFIX+r0+QB
        rows=lax.broadcasted_iota(jnp.int32,(QB,HD),0)+r0
        key=lax.broadcasted_iota(jnp.int32,(QB,QB),0)
        row=lax.broadcasted_iota(jnp.int32,(QB,QB),1)
        seen=key<=row
        qs=[];gs=[];dss=[];pbs=[]
        for j in range(4):
            q=q_ref[r0:r0+QB,j*HD:(j+1)*HD]
            g=jnp.where(rows<live,g_ref[r0:r0+QB,j*HD:(j+1)*HD].astype(jnp.float32),0.0).astype(jnp.bfloat16)
            s=dot(kj[0:nk,:],q,NT)
            dp=dot(vj[0:nk,:],g,NT)
            s=jnp.concatenate([s[:nk-QB],jnp.where(seen,s[nk-QB:],-1e30)],0)
            top=jnp.max(s,0,keepdims=True)
            e=jnp.exp((s-top)*inverse)
            p=e*(1.0/jnp.sum(e,0,keepdims=True))
            rt=jnp.sum(p*dp,0,keepdims=True)
            dss.append((p*(dp-rt)).astype(jnp.bfloat16)); pbs.append(p.astype(jnp.bfloat16)); qs.append(q); gs.append(g)
        dk_acc[0:nk,:]+=dot(jnp.concatenate(dss,1),jnp.concatenate(qs,0),NN)
        dv_acc[0:nk,:]+=dot(jnp.concatenate(pbs,1),jnp.concatenate(gs,0),NN)
        for j in range(4):
            dqT=dot(kT[:,0:nk],dss[j],NN)*inverse
            a=dqT[:HD//2]; c=dqT[HD//2:]
            co=cosT_ref[:,r0:r0+QB]; si=sinT_ref[:,r0:r0+QB]
            rot=jnp.concatenate([a*co+c*si,c*co-a*si],0)
            col=pl.multiple_of((h*4+j)*HD,HD)
            out_ref[r0:r0+QB,pl.ds(col,HD)]=jnp.transpose(rot).astype(jnp.bfloat16)
    @pl.when(h==GROUP//4-1)
    def _():
        dk=dk_acc[...]*inverse
        pg_ref[0]=dk[0:PREFIX]
        pg_ref[1]=dv_acc[0:PREFIX,:]
        d=dk[PREFIX:]
        out_ref[:,GROUP*HD:(GROUP+1)*HD]=(d*cos_ref[...]+pltpu.roll(d,HD//2,1)*sin_ref[...]).astype(jnp.bfloat16)
        out_ref[:,(GROUP+1)*HD:]=dv_acc[PREFIX:,:].astype(jnp.bfloat16)

def attention(prompt,lengths,queries,out_grad,key_rows,value_rows,prefix,tables):
    whole=lambda shape: pl.BlockSpec(shape,lambda h:(0,)*len(shape))
    return pl.pallas_call(
        functools.partial(attn_kernel,prompt=prompt),
        grid=(GROUP//4,),
        in_specs=[pl.BlockSpec(memory_space=pltpu.SMEM),
            pl.BlockSpec((SEQ,4*HD),lambda h:(prompt,h)),
            pl.BlockSpec((SEQ,4*HD),lambda h:(prompt,h)),
            pl.BlockSpec((SEQ,HD),lambda h:(prompt,0)),
            pl.BlockSpec((SEQ,HD),lambda h:(prompt,0)),
            whole((2,PREFIX,HD)),whole((HD//2,SEQ)),whole((HD//2,SEQ)),whole((SEQ,HD)),whole((SEQ,HD))],
        out_specs=[whole((SEQ,(GROUP+2)*HD)),whole((2,PREFIX,HD))],
        out_shape=[jax.ShapeDtypeStruct((SEQ,(GROUP+2)*HD),jnp.bfloat16),jax.ShapeDtypeStruct((2,PREFIX,HD),jnp.float32)],
        scratch_shapes=[pltpu.VMEM((PREFIX+SEQ,HD),jnp.bfloat16),pltpu.VMEM((PREFIX+SEQ,HD),jnp.bfloat16),pltpu.VMEM((HD,PREFIX+SEQ),jnp.bfloat16),
            pltpu.VMEM((PREFIX+SEQ,HD),jnp.float32),pltpu.VMEM((PREFIX+SEQ,HD),jnp.float32)],
        compiler_params=pltpu.CompilerParams(vmem_limit_bytes=58*2**20),
        cost_estimate=pl.CostEstimate(flops=5*2*8*512*576*128,bytes_accessed=4*2**20,transcendentals=8*512*576),
        name="attention_backward",
    )(lengths,queries,out_grad,key_rows,value_rows,prefix,*tables)


AXES = ("x", "y", "z", "c")


def pairs_of(move):
    def flat(x, y, z, c):
        return ((x * 4 + y) * 4 + z) * 2 + c

    found = []
    for x in range(4):
        for y in range(4):
            for z in range(4):
                for c in range(2):
                    target = move(x, y, z, c)
                    if target is not None:
                        found.append((flat(x, y, z, c), flat(*target)))
    return found


def send(array, move):
    return lax.ppermute(array, AXES, pairs_of(move))


def x_mate(x, y, z, c):
    return (x ^ 1, y, z, c)


def x_cross(x, y, z, c):
    return (3 - x, y, z, c)


def x_side(x, y, z, c):
    return (x ^ 1 if c == 0 else 3 - x, y, z, c)


def x_side_other(x, y, z, c):
    return (x ^ 1 if c == 1 else 3 - x, y, z, 1 - c)


def x_turn(x, y, z, c):
    return (3 - x if c == 0 else x ^ 1, y, z, c)


def y_mate(x, y, z, c):
    return (x, y ^ 1, z, c)


def y_partner(x, y, z, c):
    return (x, 3 - y, z, c)


def z_side(x, y, z, c):
    return (x, y, z ^ 1 if c == 0 else 3 - z, c)


def z_turn(x, y, z, c):
    return (x, y, 3 - z if c == 0 else z ^ 1, c)


def sibling(x, y, z, c):
    return (x, y, z, 1 - c)


def home_same(x, y, z, c):
    return (x, 3 - y, z, c) if c == y // 2 else None


def home_other(x, y, z, c):
    return (x, 3 - y, z, 1 - c) if c != y // 2 else None


def project_kernel(plan, n_arrays, *refs):
    sides, groups, outs_of = plan
    arrays, rest = refs[:n_arrays], refs[n_arrays:]
    outs, left, right, made, sems = rest[: 2 * outs_of], *rest[2 * outs_of :]
    cols, width = right.shape[1], right.shape[2] // 2
    rows = left.shape[0] // len(sides)
    places = arrays[0]
    sem = iter(range(sems.shape[0]))

    def begin(source, target):
        copy = pltpu.make_async_copy(source, target, sems.at[next(sem)])
        copy.start()
        return copy

    def load_side(n):
        return [
            begin(arrays[at], left.at[n * rows : (n + 1) * rows, part * width : (part + 1) * width])
            for part, at in enumerate(sides[n])
        ]

    side_loads = load_side(0)
    blocks = [pair for group, _ in groups for pair in group]
    block_loads = [
        [
            begin(arrays[at].at[row : row + cols], right.at[slot, :, part * width : (part + 1) * width])
            for part, (at, row) in enumerate(pair)
        ]
        for slot, pair in enumerate(blocks)
    ]
    for n in range(1, len(sides)):
        side_loads += load_side(n)
    slot, done, ready, stores = 0, 0, set(), []
    for group, (first, last, cuts) in groups:
        for unit in range(first, last):
            waits = [] if unit in ready else side_loads[2 * unit : 2 * unit + 2]
            ready.add(unit)
            for index in range(len(group)):
                for copy in waits + (block_loads[slot + index] if unit == first else []):
                    copy.wait()
                waits = []
                for cut in range(0, rows, 256):
                    total = dot(left[unit * rows + cut : unit * rows + cut + 256], right[slot + index], NT)
                    made[places[index], done + cut : done + cut + 256] = total.astype(jnp.bfloat16)
            out, row = cuts[unit - first]
            for part in range(2):
                stores.append(
                    begin(made.at[2 * part : 2 * part + 2, done : done + rows], outs[2 * out + part].at[:, row : row + rows])
                )
            done += rows
        slot += len(group)
    for copy in stores:
        copy.wait()


def project(places, groups, cols=256):
    arrays, kinds = [places], [pltpu.SMEM]

    def slot_of(array):
        for at, known in enumerate(arrays):
            if known is array:
                return at
        arrays.append(array)
        kinds.append(pl.ANY)
        return len(arrays) - 1

    sides, plan, out_rows, total = [], [], {}, 0
    for blocks, lhs, cuts in groups:
        pairs = [tuple((slot_of(array), row) for array, row in pair) for pair in blocks]
        found = [(slot_of(own), slot_of(other)) for own, other in lhs]
        for side in found:
            if side not in sides:
                sides.append(side)
        for (own, _), (out, row) in zip(lhs, cuts):
            out_rows[out] = max(out_rows.get(out, 0), row + own.shape[0])
            total += own.shape[0]
        first = sides.index(found[0])
        plan.append((pairs, (first, first + len(found), cuts)))
    rows, width = arrays[sides[0][0]].shape
    n_blocks = sum(len(pairs) for pairs, _ in plan)
    hbm = pl.BlockSpec(memory_space=pl.ANY)
    out = pl.pallas_call(
        functools.partial(project_kernel, (sides, plan, len(out_rows)), len(arrays)),
        in_specs=[pl.BlockSpec(memory_space=kind) for kind in kinds],
        out_specs=[hbm] * (2 * len(out_rows)),
        out_shape=[jax.ShapeDtypeStruct((2, out_rows[at], cols), jnp.bfloat16) for at in sorted(out_rows) for _ in range(2)],
        scratch_shapes=[
            pltpu.VMEM((len(sides) * rows, 2 * width), jnp.bfloat16),
            pltpu.VMEM((n_blocks, cols, 2 * width), jnp.bfloat16),
            pltpu.VMEM((4, total, cols), jnp.bfloat16),
            pltpu.SemaphoreType.DMA((2 * len(sides) + 2 * n_blocks + 2 * (total // rows),)),
        ],
        compiler_params=pltpu.CompilerParams(vmem_limit_bytes=58 * 2**20),
        name="project",
    )(*arrays)
    return [(out[2 * at], out[2 * at + 1]) for at in range(len(out_rows))]


def arrange_kernel(info, near, mate, near_in, mate_in, same0, same1, other0, other1, out_ref, sems):
    at_home, near_at, own_at = info[0], info[1], info[2]
    size = near.shape[1]

    def put(pieces):
        copies = []
        for value, row, base, core_at in pieces:
            col = pl.multiple_of(base * 512 + core_at * 256, 256)
            target = out_ref.at[row * size : (row + 1) * size, pl.ds(col, 256)]
            copies.append(pltpu.make_async_copy(value, target, sems.at[len(copies)]))
            copies[-1].start()
        for copy in copies:
            copy.wait()

    @pl.when(at_home == 1)
    def _():
        pieces = []
        for row in range(2):
            pieces += [(near.at[row], row, near_at, own_at), (mate.at[row], row, 1 - near_at, own_at)]
            pieces += [(near_in.at[row], row, near_at, 1 - own_at), (mate_in.at[row], row, 1 - near_at, 1 - own_at)]
        put(pieces)

    @pl.when(at_home == 0)
    def _():
        pieces = []
        for row, (same, other) in enumerate(((same0, other0), (same1, other1))):
            pieces += [(same.at[0], row, near_at, own_at), (same.at[1], row, 1 - near_at, own_at)]
            pieces += [(other.at[0], row, near_at, 1 - own_at), (other.at[1], row, 1 - near_at, 1 - own_at)]
        put(pieces)


def arrange(info, *parts):
    hbm = pl.BlockSpec(memory_space=pl.ANY)
    return pl.pallas_call(
        arrange_kernel,
        in_specs=[pl.BlockSpec(memory_space=pltpu.SMEM)] + [hbm] * 8,
        out_specs=pl.BlockSpec(memory_space=pltpu.VMEM),
        out_shape=jax.ShapeDtypeStruct((1024, 1024), jnp.bfloat16),
        scratch_shapes=[pltpu.SemaphoreType.DMA((8,))],
        compiler_params=pltpu.CompilerParams(vmem_limit_bytes=58 * 2**20),
        name="arrange",
    )(info, *parts)


def wide(array):
    return array.astype(jnp.float32)


def body(queries, key_rows, value_rows, out_grad, prefix, lengths, qkv_weight):
    gate = lax.optimization_barrier
    x_at, y_at, z_at, core = (lax.axis_index(a) for a in AXES)
    half = y_at // 2
    rows = qkv_weight.shape[0] // 2
    tables = tuple(jnp.asarray(t) for t in rope_tables())
    x_first, x_second = jnp.where(core == 0, x_at ^ 1, 3 - x_at), jnp.where(core == 0, 3 - x_at, x_at ^ 1)
    z_first, z_second = jnp.where(core == 0, z_at ^ 1, 3 - z_at), jnp.where(core == 0, 3 - z_at, z_at ^ 1)
    targets = jnp.stack([x_at, x_first, x_second, x_at ^ 2]).astype(jnp.int32)
    places = jnp.where(
        targets == z_at, 0, jnp.where(targets == z_second, 1, jnp.where(targets == z_first, 2, 3))
    ).astype(jnp.int32)

    kept = lax.dynamic_slice_in_dim(qkv_weight, core * rows, rows, 0)
    given = lax.dynamic_slice_in_dim(qkv_weight, (1 - core) * rows, rows, 0)
    kept, given, places = gate((kept, given, places))

    side_a = send(kept, x_side)
    side_b = send(given, x_side_other)
    taken = send(given, sibling)
    self0, terms0 = attention(0, lengths, queries, out_grad, key_rows, value_rows, prefix, tables)
    side_a, side_b, taken, self0, terms0, key_rows, kept = gate((side_a, side_b, taken, self0, terms0, key_rows, kept))
    mine = jnp.concatenate([kept, taken], 0)
    turned = send(jnp.concatenate([kept, taken, side_a, side_b], 0), x_turn)
    mate = send(mine, y_mate)
    pair0 = send(self0, y_partner)
    self0_other = send(self0, sibling)
    self1, terms1 = attention(1, lengths, queries, out_grad, key_rows, value_rows, prefix, tables)
    count_row = jnp.full((8, HD), jnp.sum(lengths).astype(jnp.float32))
    turned, mate, pair0, self0_other, self1, terms1, terms0, mine, self0 = gate(
        (turned, mate, pair0, self0_other, self1, terms1, terms0, mine, self0)
    )
    near_blocks = [
        ((mine, 0), (mine, rows)),
        ((side_a, 0), (side_b, 0)),
        ((turned, 0), (turned, rows)),
        ((turned, 2 * rows), (turned, 3 * rows)),
    ]

    def start_unit(partial):
        keep, give = partial
        return keep, send(give, z_side)

    def pass_on(held):
        partial, arrived = held
        total = (wide(partial[1]) + wide(arrived[1])).astype(jnp.bfloat16)
        return partial, arrived, send(total, z_turn)

    def finish(held):
        partial, arrived, last = held
        return ((wide(partial[0]) + wide(arrived[0]) + wide(last)) * loss_scale).astype(jnp.bfloat16)

    self1_other = send(self1, sibling)
    pair0_other = send(pair0, sibling)
    mate_side = send(mate, x_side)
    mate_turn = send(mate, x_turn)
    mate_far = send(turned[2 * rows :], y_mate)
    pair1 = send(self1, y_partner)
    both0, both1, there0 = (self0, self0_other), (self1, self1_other), (pair0, pair0_other)
    early = project(places, [(near_blocks, [both0, both1, there0], [(0, 0), (0, SEQ), (0, 2 * SEQ)])])[0]
    mate_side, mate_turn, mate_far, pair1, there0, both0, both1, early, mate, terms0, terms1 = gate(
        (mate_side, mate_turn, mate_far, pair1, there0, both0, both1, early, mate, terms0, terms1)
    )
    mate_blocks = [((array, 0), (array, rows)) for array in (mate, mate_side, mate_turn, mate_far)]
    pair1_other = send(pair1, sibling)
    early = start_unit(early)
    terms = jnp.concatenate([(terms0 + terms1).reshape(2 * PREFIX, HD), count_row], 0)
    terms = terms + send(terms, x_mate)
    p0m, sm = project(places, [(mate_blocks, [there0, both0, both1], [(0, 0), (1, 0), (1, SEQ)])])
    pair1_other, early, p0m, pair1, terms, sm = gate((pair1_other, early, p0m, pair1, terms, sm))
    early, p0m = pass_on(early), start_unit(p0m)
    there1 = (pair1, pair1_other)
    terms = terms + send(terms, x_cross)
    p1 = project(places, [(near_blocks, [there1], [(0, 0)]), (mate_blocks, [there1], [(0, SEQ)])])[0]
    early, p0m, p1, terms, sm = gate((early, p0m, p1, terms, sm))
    p0m, p1 = pass_on(p0m), start_unit(p1)
    terms = terms + send(terms, y_mate)
    terms = terms + send(terms, y_partner)
    p0m, p1, terms, early, sm = gate((p0m, p1, terms, early, sm))
    loss_scale = 16384.0 / terms[2 * PREFIX, 0]
    p1, sm = pass_on(p1), start_unit(sm)
    early = finish(early)
    near = early[: 2 * SEQ].reshape(2, SEQ, 256)
    pair0 = jnp.stack([early[2 * SEQ :], finish(p0m)])
    same0, other0 = send(pair0, home_same), send(pair0, home_other)
    near_in = send(near, sibling)
    near_in, same0, other0, p1, sm, loss_scale, near = gate((near_in, same0, other0, p1, sm, loss_scale, near))
    pair1 = finish(p1).reshape(2, SEQ, 256)
    same1, other1 = send(pair1, home_same), send(pair1, home_other)
    sm = pass_on(sm)
    mate = finish(sm).reshape(2, SEQ, 256)
    mate_in = send(mate, sibling)
    at_home = core == half
    near_at = jnp.where(at_home, y_at % 2, 1 - y_at % 2)
    info = jnp.stack([at_home.astype(jnp.int32), near_at, core]).astype(jnp.int32)
    input_grad = arrange(info, near, mate, near_in, mate_in, same0, same1, other0, other1)
    new_prefix = prefix - learning_rate * loss_scale * terms[: 2 * PREFIX].reshape(2, PREFIX, HD)
    return (input_grad, new_prefix)


def solution(mesh):
    fine = Mesh(mesh.devices.reshape(4, 4, 4, 2), AXES)
    dp, tensor = ("x", "y"), ("z", "c")
    both = P(dp, tensor)
    return jax.shard_map(
        body,
        mesh=fine,
        in_specs=(both, both, both, both, P(None, None, tensor), P(dp), both),
        out_specs=(both, P(None, None, tensor)),
        check_vma=False,
    )
```

```python
import functools
import math

import jax
import jax.numpy as jnp
import numpy as np
from jax import lax
from jax.experimental import pallas as pl
from jax.experimental.pallas import tpu as pltpu
from jax.sharding import Mesh
from jax.sharding import PartitionSpec as P

learning_rate = 0.1

HD=128; GROUP=8; PREFIX=64; SEQ=512; QB=256
rope_base=500000.0

def rope_tables():
    half=HD//2
    freq=np.power(rope_base,-(2.0*np.arange(half))/HD).astype(np.float32)
    ang=(np.arange(SEQ,dtype=np.float32)[:,None]*freq[None,:]).astype(np.float64)
    cos,sin=np.cos(ang).astype(np.float32),np.sin(ang).astype(np.float32)
    wide_cos=np.concatenate([cos,cos],1)
    wide_sin=np.concatenate([sin,-sin],1)
    return cos.T.copy(),sin.T.copy(),wide_cos,wide_sin

NT=(((1,),(1,)),((),()))
NN=(((1,),(0,)),((),()))
def dot(a,b,dims): return lax.dot_general(a,b,dims,preferred_element_type=jnp.float32)

def attn_kernel(len_ref,q_ref,g_ref,k_ref,v_ref,pre_ref,cosT_ref,sinT_ref,cos_ref,sin_ref,out_ref,pg_ref,kj,vj,kT,dk_acc,dv_acc,*,prompt):
    h=pl.program_id(0)
    inverse=1.0/math.sqrt(HD)
    @pl.when(h==0)
    def _():
        kj[0:PREFIX,:]=pre_ref[0].astype(jnp.bfloat16)
        vj[0:PREFIX,:]=pre_ref[1].astype(jnp.bfloat16)
        kj[PREFIX:,:]=k_ref[...]
        vj[PREFIX:,:]=v_ref[...]
        kT[...]=jnp.transpose(kj[...].astype(jnp.float32)).astype(jnp.bfloat16)
        dk_acc[...]=jnp.zeros_like(dk_acc)
        dv_acc[...]=jnp.zeros_like(dv_acc)
    live=len_ref[prompt]
    for b in range(SEQ//QB):
        r0=b*QB; nk=PREFIX+r0+QB
        rows=lax.broadcasted_iota(jnp.int32,(QB,HD),0)+r0
        key=lax.broadcasted_iota(jnp.int32,(QB,QB),0)
        row=lax.broadcasted_iota(jnp.int32,(QB,QB),1)
        seen=key<=row
        qs=[];gs=[];dss=[];pbs=[]
        for j in range(4):
            q=q_ref[r0:r0+QB,j*HD:(j+1)*HD]
            g=jnp.where(rows<live,g_ref[r0:r0+QB,j*HD:(j+1)*HD].astype(jnp.float32),0.0).astype(jnp.bfloat16)
            s=dot(kj[0:nk,:],q,NT)
            dp=dot(vj[0:nk,:],g,NT)
            s=jnp.concatenate([s[:nk-QB],jnp.where(seen,s[nk-QB:],-1e30)],0)
            top=jnp.max(s,0,keepdims=True)
            e=jnp.exp((s-top)*inverse)
            p=e*(1.0/jnp.sum(e,0,keepdims=True))
            rt=jnp.sum(p*dp,0,keepdims=True)
            dss.append((p*(dp-rt)).astype(jnp.bfloat16)); pbs.append(p.astype(jnp.bfloat16)); qs.append(q); gs.append(g)
        dk_acc[0:nk,:]+=dot(jnp.concatenate(dss,1),jnp.concatenate(qs,0),NN)
        dv_acc[0:nk,:]+=dot(jnp.concatenate(pbs,1),jnp.concatenate(gs,0),NN)
        for j in range(4):
            dqT=dot(kT[:,0:nk],dss[j],NN)*inverse
            a=dqT[:HD//2]; c=dqT[HD//2:]
            co=cosT_ref[:,r0:r0+QB]; si=sinT_ref[:,r0:r0+QB]
            rot=jnp.concatenate([a*co+c*si,c*co-a*si],0)
            col=pl.multiple_of((h*4+j)*HD,HD)
            out_ref[r0:r0+QB,pl.ds(col,HD)]=jnp.transpose(rot).astype(jnp.bfloat16)
    @pl.when(h==GROUP//4-1)
    def _():
        dk=dk_acc[...]*inverse
        pg_ref[0]=dk[0:PREFIX]
        pg_ref[1]=dv_acc[0:PREFIX,:]
        d=dk[PREFIX:]
        out_ref[:,GROUP*HD:(GROUP+1)*HD]=(d*cos_ref[...]+pltpu.roll(d,HD//2,1)*sin_ref[...]).astype(jnp.bfloat16)
        out_ref[:,(GROUP+1)*HD:]=dv_acc[PREFIX:,:].astype(jnp.bfloat16)

def attention(prompt,lengths,queries,out_grad,key_rows,value_rows,prefix,tables):
    whole=lambda shape: pl.BlockSpec(shape,lambda h:(0,)*len(shape))
    return pl.pallas_call(
        functools.partial(attn_kernel,prompt=prompt),
        grid=(GROUP//4,),
        in_specs=[pl.BlockSpec(memory_space=pltpu.SMEM),
            pl.BlockSpec((SEQ,4*HD),lambda h:(prompt,h)),
            pl.BlockSpec((SEQ,4*HD),lambda h:(prompt,h)),
            pl.BlockSpec((SEQ,HD),lambda h:(prompt,0)),
            pl.BlockSpec((SEQ,HD),lambda h:(prompt,0)),
            whole((2,PREFIX,HD)),whole((HD//2,SEQ)),whole((HD//2,SEQ)),whole((SEQ,HD)),whole((SEQ,HD))],
        out_specs=[whole((SEQ,(GROUP+2)*HD)),whole((2,PREFIX,HD))],
        out_shape=[jax.ShapeDtypeStruct((SEQ,(GROUP+2)*HD),jnp.bfloat16),jax.ShapeDtypeStruct((2,PREFIX,HD),jnp.float32)],
        scratch_shapes=[pltpu.VMEM((PREFIX+SEQ,HD),jnp.bfloat16),pltpu.VMEM((PREFIX+SEQ,HD),jnp.bfloat16),pltpu.VMEM((HD,PREFIX+SEQ),jnp.bfloat16),
            pltpu.VMEM((PREFIX+SEQ,HD),jnp.float32),pltpu.VMEM((PREFIX+SEQ,HD),jnp.float32)],
        compiler_params=pltpu.CompilerParams(vmem_limit_bytes=58*2**20),
        cost_estimate=pl.CostEstimate(flops=5*2*8*512*576*128,bytes_accessed=4*2**20,transcendentals=8*512*576),
        name="attention_backward",
    )(lengths,queries,out_grad,key_rows,value_rows,prefix,*tables)


AXES = ("x", "y", "z", "c")


def pairs_of(move):
    def flat(x, y, z, c):
        return ((x * 4 + y) * 4 + z) * 2 + c

    found = []
    for x in range(4):
        for y in range(4):
            for z in range(4):
                for c in range(2):
                    target = move(x, y, z, c)
                    if target is not None:
                        found.append((flat(x, y, z, c), flat(*target)))
    return found


def send(array, move):
    return lax.ppermute(array, AXES, pairs_of(move))


def x_mate(x, y, z, c):
    return (x ^ 1, y, z, c)


def x_cross(x, y, z, c):
    return (3 - x, y, z, c)


def x_side(x, y, z, c):
    return (x ^ 1 if c == 0 else 3 - x, y, z, c)


def x_side_other(x, y, z, c):
    return (x ^ 1 if c == 1 else 3 - x, y, z, 1 - c)


def x_turn(x, y, z, c):
    return (3 - x if c == 0 else x ^ 1, y, z, c)


def y_mate(x, y, z, c):
    return (x, y ^ 1, z, c)


def y_partner(x, y, z, c):
    return (x, 3 - y, z, c)


def z_side(x, y, z, c):
    return (x, y, z ^ 1 if c == 0 else 3 - z, c)


def z_turn(x, y, z, c):
    return (x, y, 3 - z if c == 0 else z ^ 1, c)


def sibling(x, y, z, c):
    return (x, y, z, 1 - c)


def home_same(x, y, z, c):
    return (x, 3 - y, z, c) if c == y // 2 else None


def home_other(x, y, z, c):
    return (x, 3 - y, z, 1 - c) if c != y // 2 else None


def project_kernel(plan, n_arrays, *refs):
    sides, groups, outs_of = plan
    arrays, rest = refs[:n_arrays], refs[n_arrays:]
    outs, left, right, made, sems = rest[: 2 * outs_of], *rest[2 * outs_of :]
    cols, width = right.shape[1], right.shape[2] // 2
    rows = left.shape[0] // len(sides)
    places = arrays[0]
    sem = iter(range(sems.shape[0]))

    def begin(source, target):
        copy = pltpu.make_async_copy(source, target, sems.at[next(sem)])
        copy.start()
        return copy

    def load_side(n):
        return [
            begin(arrays[at], left.at[n * rows : (n + 1) * rows, part * width : (part + 1) * width])
            for part, at in enumerate(sides[n])
        ]

    side_loads = load_side(0)
    blocks = [pair for group, _ in groups for pair in group]
    block_loads = [
        [
            begin(arrays[at].at[row : row + cols], right.at[slot, :, part * width : (part + 1) * width])
            for part, (at, row) in enumerate(pair)
        ]
        for slot, pair in enumerate(blocks)
    ]
    for n in range(1, len(sides)):
        side_loads += load_side(n)
    slot, done, ready, stores = 0, 0, set(), []
    for group, (first, last, cuts) in groups:
        for unit in range(first, last):
            waits = [] if unit in ready else side_loads[2 * unit : 2 * unit + 2]
            ready.add(unit)
            for index in range(len(group)):
                for copy in waits + (block_loads[slot + index] if unit == first else []):
                    copy.wait()
                waits = []
                for cut in range(0, rows, 256):
                    total = dot(left[unit * rows + cut : unit * rows + cut + 256], right[slot + index], NT)
                    made[places[index], done + cut : done + cut + 256] = total.astype(jnp.bfloat16)
            out, row = cuts[unit - first]
            for part in range(2):
                stores.append(
                    begin(made.at[2 * part : 2 * part + 2, done : done + rows], outs[2 * out + part].at[:, row : row + rows])
                )
            done += rows
        slot += len(group)
    for copy in stores:
        copy.wait()


def project(places, groups, cols=256):
    arrays, kinds = [places], [pltpu.SMEM]

    def slot_of(array):
        for at, known in enumerate(arrays):
            if known is array:
                return at
        arrays.append(array)
        kinds.append(pl.ANY)
        return len(arrays) - 1

    sides, plan, out_rows, total = [], [], {}, 0
    for blocks, lhs, cuts in groups:
        pairs = [tuple((slot_of(array), row) for array, row in pair) for pair in blocks]
        found = [(slot_of(own), slot_of(other)) for own, other in lhs]
        for side in found:
            if side not in sides:
                sides.append(side)
        for (own, _), (out, row) in zip(lhs, cuts):
            out_rows[out] = max(out_rows.get(out, 0), row + own.shape[0])
            total += own.shape[0]
        first = sides.index(found[0])
        plan.append((pairs, (first, first + len(found), cuts)))
    rows, width = arrays[sides[0][0]].shape
    n_blocks = sum(len(pairs) for pairs, _ in plan)
    hbm = pl.BlockSpec(memory_space=pl.ANY)
    out = pl.pallas_call(
        functools.partial(project_kernel, (sides, plan, len(out_rows)), len(arrays)),
        in_specs=[pl.BlockSpec(memory_space=kind) for kind in kinds],
        out_specs=[hbm] * (2 * len(out_rows)),
        out_shape=[jax.ShapeDtypeStruct((2, out_rows[at], cols), jnp.bfloat16) for at in sorted(out_rows) for _ in range(2)],
        scratch_shapes=[
            pltpu.VMEM((len(sides) * rows, 2 * width), jnp.bfloat16),
            pltpu.VMEM((n_blocks, cols, 2 * width), jnp.bfloat16),
            pltpu.VMEM((4, total, cols), jnp.bfloat16),
            pltpu.SemaphoreType.DMA((2 * len(sides) + 2 * n_blocks + 2 * (total // rows),)),
        ],
        compiler_params=pltpu.CompilerParams(vmem_limit_bytes=58 * 2**20),
        name="project",
    )(*arrays)
    return [(out[2 * at], out[2 * at + 1]) for at in range(len(out_rows))]


def arrange_kernel(info, near, mate, near_in, mate_in, same0, same1, other0, other1, out_ref, sems):
    at_home, near_at, own_at = info[0], info[1], info[2]
    size = near.shape[1]

    def put(pieces):
        copies = []
        for value, row, base, core_at in pieces:
            col = pl.multiple_of(base * 512 + core_at * 256, 256)
            target = out_ref.at[row * size : (row + 1) * size, pl.ds(col, 256)]
            copies.append(pltpu.make_async_copy(value, target, sems.at[len(copies)]))
            copies[-1].start()
        for copy in copies:
            copy.wait()

    @pl.when(at_home == 1)
    def _():
        pieces = []
        for row in range(2):
            pieces += [(near.at[row], row, near_at, own_at), (mate.at[row], row, 1 - near_at, own_at)]
            pieces += [(near_in.at[row], row, near_at, 1 - own_at), (mate_in.at[row], row, 1 - near_at, 1 - own_at)]
        put(pieces)

    @pl.when(at_home == 0)
    def _():
        pieces = []
        for row, (same, other) in enumerate(((same0, other0), (same1, other1))):
            pieces += [(same.at[0], row, near_at, own_at), (same.at[1], row, 1 - near_at, own_at)]
            pieces += [(other.at[0], row, near_at, 1 - own_at), (other.at[1], row, 1 - near_at, 1 - own_at)]
        put(pieces)


def arrange(info, *parts):
    hbm = pl.BlockSpec(memory_space=pl.ANY)
    return pl.pallas_call(
        arrange_kernel,
        in_specs=[pl.BlockSpec(memory_space=pltpu.SMEM)] + [hbm] * 8,
        out_specs=pl.BlockSpec(memory_space=pltpu.VMEM),
        out_shape=jax.ShapeDtypeStruct((1024, 1024), jnp.bfloat16),
        scratch_shapes=[pltpu.SemaphoreType.DMA((8,))],
        compiler_params=pltpu.CompilerParams(vmem_limit_bytes=58 * 2**20),
        name="arrange",
    )(info, *parts)


def wide(array):
    return array.astype(jnp.float32)


def body(queries, key_rows, value_rows, out_grad, prefix, lengths, qkv_weight):
    gate = lax.optimization_barrier
    x_at, y_at, z_at, core = (lax.axis_index(a) for a in AXES)
    half = y_at // 2
    rows = qkv_weight.shape[0] // 2
    tables = tuple(jnp.asarray(t) for t in rope_tables())
    x_first, x_second = jnp.where(core == 0, x_at ^ 1, 3 - x_at), jnp.where(core == 0, 3 - x_at, x_at ^ 1)
    z_first, z_second = jnp.where(core == 0, z_at ^ 1, 3 - z_at), jnp.where(core == 0, 3 - z_at, z_at ^ 1)
    targets = jnp.stack([x_at, x_first, x_second, x_at ^ 2]).astype(jnp.int32)
    places = jnp.where(
        targets == z_at, 0, jnp.where(targets == z_second, 1, jnp.where(targets == z_first, 2, 3))
    ).astype(jnp.int32)

    kept = lax.dynamic_slice_in_dim(qkv_weight, core * rows, rows, 0)
    given = lax.dynamic_slice_in_dim(qkv_weight, (1 - core) * rows, rows, 0)
    kept, given, places = gate((kept, given, places))

    side_a = send(kept, x_side)
    side_b = send(given, x_side_other)
    taken = send(given, sibling)
    self0, terms0 = attention(0, lengths, queries, out_grad, key_rows, value_rows, prefix, tables)
    side_a, side_b, taken, self0, terms0, key_rows, kept = gate((side_a, side_b, taken, self0, terms0, key_rows, kept))
    mine = jnp.concatenate([kept, taken], 0)
    turned = send(mine, x_turn)
    turned_far = send(jnp.concatenate([side_a, side_b], 0), x_turn)
    mate = send(mine, y_mate)
    pair0 = send(self0, y_partner)
    self0_other = send(self0, sibling)
    self1, terms1 = attention(1, lengths, queries, out_grad, key_rows, value_rows, prefix, tables)
    count_row = jnp.full((8, HD), jnp.sum(lengths).astype(jnp.float32))
    turned, turned_far, mate, pair0, self0_other, self1, terms1, terms0, mine, self0 = gate(
        (turned, turned_far, mate, pair0, self0_other, self1, terms1, terms0, mine, self0)
    )
    near_blocks = [
        ((mine, 0), (mine, rows)),
        ((side_a, 0), (side_b, 0)),
        ((turned, 0), (turned, rows)),
        ((turned_far, 0), (turned_far, rows)),
    ]

    def start_unit(partial):
        keep, give = partial
        return keep, send(give, z_side)

    def pass_on(held):
        partial, arrived = held
        total = (wide(partial[1]) + wide(arrived[1])).astype(jnp.bfloat16)
        return partial, arrived, send(total, z_turn)

    def finish(held):
        partial, arrived, last = held
        return ((wide(partial[0]) + wide(arrived[0]) + wide(last)) * loss_scale).astype(jnp.bfloat16)

    self1_other = send(self1, sibling)
    pair0_other = send(pair0, sibling)
    mate_side = send(mate, x_side)
    mate_turn = send(mate, x_turn)
    mate_far = send(turned_far, y_mate)
    pair1 = send(self1, y_partner)
    both0, both1, there0 = (self0, self0_other), (self1, self1_other), (pair0, pair0_other)
    early = project(places, [(near_blocks, [both0, both1, there0], [(0, 0), (0, SEQ), (0, 2 * SEQ)])])[0]
    mate_side, mate_turn, mate_far, pair1, there0, both0, both1, early, mate, terms0, terms1 = gate(
        (mate_side, mate_turn, mate_far, pair1, there0, both0, both1, early, mate, terms0, terms1)
    )
    mate_blocks = [((array, 0), (array, rows)) for array in (mate, mate_side, mate_turn, mate_far)]
    pair1_other = send(pair1, sibling)
    early = start_unit(early)
    terms = jnp.concatenate([(terms0 + terms1).reshape(2 * PREFIX, HD), count_row], 0)
    terms = terms + send(terms, x_mate)
    p0m, sm = project(places, [(mate_blocks, [there0, both0, both1], [(0, 0), (1, 0), (1, SEQ)])])
    pair1_other, early, p0m, pair1, terms, sm = gate((pair1_other, early, p0m, pair1, terms, sm))
    early, p0m = pass_on(early), start_unit(p0m)
    there1 = (pair1, pair1_other)
    terms = terms + send(terms, x_cross)
    p1 = project(places, [(near_blocks, [there1], [(0, 0)]), (mate_blocks, [there1], [(0, SEQ)])])[0]
    early, p0m, p1, terms, sm = gate((early, p0m, p1, terms, sm))
    p0m, p1 = pass_on(p0m), start_unit(p1)
    terms = terms + send(terms, y_mate)
    terms = terms + send(terms, y_partner)
    p0m, p1, terms, early, sm = gate((p0m, p1, terms, early, sm))
    loss_scale = 16384.0 / terms[2 * PREFIX, 0]
    p1, sm = pass_on(p1), start_unit(sm)
    early = finish(early)
    near = early[: 2 * SEQ].reshape(2, SEQ, 256)
    pair0 = jnp.stack([early[2 * SEQ :], finish(p0m)])
    same0, other0 = send(pair0, home_same), send(pair0, home_other)
    near_in = send(near, sibling)
    near_in, same0, other0, p1, sm, loss_scale, near = gate((near_in, same0, other0, p1, sm, loss_scale, near))
    pair1 = finish(p1).reshape(2, SEQ, 256)
    same1, other1 = send(pair1, home_same), send(pair1, home_other)
    sm = pass_on(sm)
    mate = finish(sm).reshape(2, SEQ, 256)
    mate_in = send(mate, sibling)
    at_home = core == half
    near_at = jnp.where(at_home, y_at % 2, 1 - y_at % 2)
    info = jnp.stack([at_home.astype(jnp.int32), near_at, core]).astype(jnp.int32)
    input_grad = arrange(info, near, mate, near_in, mate_in, same0, same1, other0, other1)
    new_prefix = prefix - learning_rate * loss_scale * terms[: 2 * PREFIX].reshape(2, PREFIX, HD)
    return (input_grad, new_prefix)


def solution(mesh):
    fine = Mesh(mesh.devices.reshape(4, 4, 4, 2), AXES)
    dp, tensor = ("x", "y"), ("z", "c")
    both = P(dp, tensor)
    return jax.shard_map(
        body,
        mesh=fine,
        in_specs=(both, both, both, both, P(None, None, tensor), P(dp), both),
        out_specs=(both, P(None, None, tensor)),
        check_vma=False,
    )
```
